32 devices in a mesh: ctx: 16 (over z, y, x), fsdp: 2 (over core).
Axes of the slice: x: 2, y: 2, z: 4, core: 2. Of those that a mesh axis runs over, the one named last changes fastest.
Arguments:
- x_in: bfloat16 [4, 1024, 576], P('fsdp', 'ctx')
- w_query: bfloat16 [576, 576], P('fsdp'), may hold values from -0.25 to 0.25
- w_key: bfloat16 [576, 192], P('fsdp'), may hold values from -0.25 to 0.25
- w_value: bfloat16 [576, 192], P('fsdp'), may hold values from -0.25 to 0.25
- w_out: bfloat16 [576, 576], P('fsdp'), may hold values from -6 to 6
- attn_gain: bfloat16 [576], P('fsdp'), may hold values from 0.5 to 1.5
- w_gate: bfloat16 [576, 1536], P('fsdp'), may hold values from -0.25 to 0.25
- w_up: bfloat16 [576, 1536], P('fsdp'), may hold values from -0.25 to 0.25
- w_down: bfloat16 [1536, 576], P('fsdp'), may hold values from -0.15625 to 0.15625
- mlp_gain: bfloat16 [576], P('fsdp'), may hold values from 0.5 to 1.5
- block_of_slot: int32 [32], replicated, may hold values from 0 to 31, as said below
- out_grad: bfloat16 [4, 1024, 576], P('fsdp', 'ctx'), may hold values from -6 to 6
Outputs:
- y_out: bfloat16 [4, 1024, 576], P('fsdp', 'ctx')
- x_grad: bfloat16 [4, 1024, 576], P('fsdp', 'ctx')
- grad_w_query: float32 [576, 576], P('fsdp')
- grad_w_key: float32 [576, 192], P('fsdp')
- grad_w_value: float32 [576, 192], P('fsdp')
- grad_w_out: float32 [576, 576], P('fsdp')
- grad_attn_gain: float32 [576], P('fsdp')
- grad_w_gate: float32 [576, 1536], P('fsdp')
- grad_w_up: float32 [576, 1536], P('fsdp')
- grad_w_down: float32 [1536, 576], P('fsdp')
- grad_mlp_gain: float32 [576], P('fsdp')
The draws below stay inside these ranges and needn't reach their ends.
Inputs may be any that keep to these rules, and one draw needn't show every extreme that they name: `block_of_slot`: the entries are a permutation of 0 to 31 and entries 2 i and 2 i + 1 sum to 31, so slots 2 i and 2 i + 1 hold a block from the front of the sequence and its mirror from the back.
All inputs are finite; a program needn't handle non-finite values.
Results may differ from the reference program's by a relative error of at most 0.025.
Values may be sent and summed in bfloat16 or wider, within the bound.
A program may use at most 128 MiB of HBM per device.

```python
import math
import jax
import jax.numpy as jnp
from jax import lax

D = 576
HEADS = 9
KV_HEADS = 3
HEAD_DIM = 64
FF = 1536
BLOCK = 32
LENGTH = 1024
SEQS = 4
KV_WIDTH = 192
N_CTX = 16


def draw_x_in(key, part):
    key = jax.random.fold_in(key, 11)
    base_key, row_key, col_key = jax.random.split(key, 3)
    base = jax.random.normal(base_key, (SEQS, LENGTH, D), jnp.float32)
    row_scale = jnp.exp(jax.random.uniform(row_key, (SEQS, LENGTH, 1), jnp.float32, math.log(0.3), math.log(3.0)))
    col_scale = jnp.exp(jax.random.uniform(col_key, (D,), jnp.float32, math.log(0.5), math.log(2.0)))
    return (base * row_scale * col_scale).astype(jnp.bfloat16)


def draw_block_of_slot(key, part):
    key = jax.random.fold_in(key, 5)
    order = jax.random.permutation(key, N_CTX).astype(jnp.int32)
    mirror = 2 * N_CTX - 1 - order
    return jnp.stack([order, mirror], axis=1).reshape(2 * N_CTX).astype(jnp.int32)


def levels(key, shape, cuts, least, top_value):
    factor_of, own = 1.0, jax.random.fold_in(key, 6)
    for axis_at, blocks in cuts:
        draws = jnp.exp(jax.random.uniform(jax.random.fold_in(own, axis_at), (blocks,), jnp.float32, least / len(cuts), top_value / len(cuts)))
        factor_of = factor_of * jnp.repeat(draws, shape[axis_at] // blocks).reshape([-1 if axis == axis_at else 1 for axis in range(len(shape))])
    return factor_of


def noise(own_key, shape, deviation, reach, shards=(), held_as=jnp.bfloat16):
    drawn = jax.random.normal(own_key, shape, jnp.float32) * deviation
    if len(shards) > 0:
        drawn = levels(own_key, shape, shards, -0.22, 0.18) * drawn
    return jnp.clip(drawn, min=-reach, max=reach).astype(held_as)


def setup_inputs(seed: int = 0) -> dict:
    keys = jax.random.split(jax.random.key(seed), 13)
    return {
        "x_in": draw_x_in(jax.random.fold_in(keys[12], 71), 0),
        "w_query": noise(keys[1], (D, D), D ** -0.5, 0.25, ((0, 2),)),
        "w_key": noise(keys[2], (D, KV_WIDTH), D ** -0.5, 0.25, ((0, 2),)),
        "w_value": noise(keys[3], (D, KV_WIDTH), D ** -0.5, 0.25, ((0, 2),)),
        "w_out": noise(keys[4], (D, D), (max(1, 2 * D // LENGTH)) ** -0.5, 6.0, ((0, 2),)),
        "attn_gain": jnp.clip(1.0 + 0.1 * jax.random.normal(keys[5], (D,), jnp.float32), 0.5, 1.5).astype(jnp.bfloat16),
        "w_gate": noise(keys[6], (D, FF), D ** -0.5, 0.25, ((0, 2),)),
        "w_up": noise(keys[7], (D, FF), D ** -0.5, 0.25, ((0, 2),)),
        "w_down": noise(keys[8], (FF, D), FF ** -0.5, 0.15625, ((0, 2),)),
        "mlp_gain": jnp.clip(1.0 + 0.1 * jax.random.normal(keys[9], (D,), jnp.float32), 0.5, 1.5).astype(jnp.bfloat16),
        "block_of_slot": draw_block_of_slot(jax.random.fold_in(keys[12], 71), 0),
        "out_grad": noise(keys[11], (SEQS, LENGTH, D), 1.0, 6.0, ((0, 2), (1, 16))),
    }


@jax.custom_vjp
def low(v):
    return lax.optimization_barrier(v.astype(jnp.bfloat16)).astype(jnp.float32)

@jax.custom_vjp
def low_back(v):
    return v

def low_keep(v):
    return (low(v), None)

def low_pass(kept, grad):
    return (grad,)

def back_keep(v):
    return (v, None)

def back_low(kept, grad):
    return (low(grad),)
low.defvjp(low_keep, low_pass)
low_back.defvjp(back_keep, back_low)
epsilon = 1e-05
theta_base = 100000.0
highest = lax.Precision.HIGHEST

def make_tables(positions):
    half_dim = HEAD_DIM // 2
    frequency = theta_base ** (-2.0 * jnp.arange(half_dim, dtype=jnp.float32) / HEAD_DIM)
    angles = positions.astype(jnp.float32)[:, None] * frequency[None, :]
    return (jnp.cos(angles), jnp.sin(angles))

def rotate(values, cosine, sine):
    half_dim = values.shape[-1] // 2
    first_half = values[..., :half_dim]
    second_half = values[..., half_dim:]
    cos_rows = cosine[:, None, :]
    sin_rows = sine[:, None, :]
    return jnp.concatenate([first_half * cos_rows - second_half * sin_rows, second_half * cos_rows + first_half * sin_rows], axis=-1)

def normalize(values, gain_vec):
    return values * lax.rsqrt(lax.optimization_barrier(jnp.mean(values * values, axis=-1, keepdims=True)) + epsilon) * gain_vec

def attention(queries, key_rows, value_rows, positions):
    length = key_rows.shape[0]
    query_block = min(512, length)
    block_count = length // query_block
    group_size = HEADS // KV_HEADS
    score_scale = HEAD_DIM ** (-0.5)

    def one_block(inputs):
        query_part, query_pos = inputs
        scores = jnp.einsum('bkgd,tkd->kgbt', query_part, key_rows, precision=highest) * score_scale
        scores = low_back(jnp.where(query_pos[:, None] >= positions[None, :], scores, -1e+30))
        weights = low(jax.nn.softmax(scores, axis=-1))
        return jnp.einsum('kgbt,tkd->bkgd', weights, value_rows, precision=highest)
    outputs = lax.map(jax.checkpoint(one_block), (queries.reshape(block_count, query_block, KV_HEADS, group_size, HEAD_DIM), positions.reshape(block_count, query_block)))
    return outputs.reshape(length, HEADS * HEAD_DIM)

def layer(x_seq, params, cosine, sine, positions):
    w_query, w_key, w_value, w_out, attn_gain, w_gate, w_up, w_down, mlp_gain = params
    length = x_seq.shape[0]
    normed = low(normalize(x_seq, attn_gain))
    queries = low(rotate(low_back(jnp.dot(normed, w_query, precision=highest)).reshape(length, HEADS, HEAD_DIM), cosine, sine))
    key_rows = low(rotate(low_back(jnp.dot(normed, w_key, precision=highest)).reshape(length, KV_HEADS, HEAD_DIM), cosine, sine))
    value_rows = low(low_back(jnp.dot(normed, w_value, precision=highest))).reshape(length, KV_HEADS, HEAD_DIM)
    attended = low(low_back(attention(queries, key_rows, value_rows, positions)))
    hidden_state = x_seq + low_back(jnp.dot(attended, w_out, precision=highest))
    normed_two = low(normalize(hidden_state, mlp_gain))
    gate_vals = low_back(jnp.dot(normed_two, w_gate, precision=highest))
    up_vals = low_back(jnp.dot(normed_two, w_up, precision=highest))
    inner_rows = low(jax.nn.silu(gate_vals) * up_vals)
    return hidden_state + low_back(jnp.dot(inner_rows, w_down, precision=highest))

def reference(x_in, w_query, w_key, w_value, w_out, attn_gain, w_gate, w_up, w_down, mlp_gain, block_of_slot, out_grad):
    row_ids = jnp.arange(LENGTH, dtype=jnp.int32)
    positions = (block_of_slot[row_ids // BLOCK] * BLOCK + row_ids % BLOCK).astype(jnp.int32)
    cosine, sine = make_tables(positions)
    params = tuple((weight.astype(jnp.float32) for weight in (w_query, w_key, w_value, w_out, attn_gain, w_gate, w_up, w_down, mlp_gain)))

    def forward(x_all, param_set):

        def per_sequence(x_seq):
            return layer(x_seq, param_set, cosine, sine, positions)
        return lax.map(jax.checkpoint(per_sequence), x_all)
    y_all, pullback = jax.vjp(forward, x_in.astype(jnp.float32), params)
    x_grad, grads = pullback(out_grad.astype(jnp.float32))
    return (y_all.astype(jnp.bfloat16), x_grad.astype(jnp.bfloat16), grads[0], grads[1], grads[2], grads[3], grads[4], grads[5], grads[6], grads[7], grads[8])
```

```python
import functools

import jax
import jax.numpy as jnp
from jax import lax
from jax.experimental import pallas as pl
from jax.experimental.pallas import tpu as pltpu
from jax.sharding import PartitionSpec as P

HEADS = 9
KV_HEADS = 3
HEAD_DIM = 64
LANES = 128
CHUNKS = 3
EXTRA_ROWS = 16

epsilon = 1e-05
theta_base = 100000.0
masked_value = -1e30
MESH = pl.DeviceIdType.MESH

ORDERS = ((2, 1, 0), (1, 0, 2), (0, 2, 1))


def ctx_dims(count):
    return (count // 4, 2, 2)


class Links:
    def __init__(self, send_sem, recv_sem, dims):
        self.send_sem = send_sem
        self.recv_sem = recv_sem
        self.dims = dims
        self.me = lax.axis_index("ctx")
        self.strides = (dims[1] * dims[2], dims[2], 1)
        self.coords = tuple(
            lax.rem(lax.div(self.me, stride), size) for stride, size in zip(self.strides, dims)
        )
        self.used = 0
        self.copies = []

    def peer(self, axis, step):
        size = self.dims[axis]
        other = lax.rem(self.coords[axis] + step, size)
        return other, self.me + (other - self.coords[axis]) * self.strides[axis]

    def send(self, source, target, device_id):
        copy = pltpu.make_async_remote_copy(
            src_ref=source,
            dst_ref=target,
            send_sem=self.send_sem.at[self.used],
            recv_sem=self.recv_sem.at[self.used],
            device_id=device_id,
            device_id_type=MESH,
        )
        copy.start()
        self.used += 1
        self.copies.append(copy)
        return copy

    def finish(self):
        for copy in self.copies:
            copy.wait_send()


def greet(links, fsdp_count):
    barrier = pltpu.get_barrier_semaphore()
    total = 0
    for axis in range(3):
        for step in range(1, links.dims[axis]):
            _, device = links.peer(axis, step)
            pl.semaphore_signal(barrier, inc=1, device_id={"ctx": device}, device_id_type=MESH)
            total += 1
    mine = lax.axis_index("fsdp")
    for step in range(1, fsdp_count):
        device = lax.rem(mine + step, fsdp_count)
        pl.semaphore_signal(barrier, inc=1, device_id={"fsdp": device}, device_id_type=MESH)
        total += 1
    pl.semaphore_wait(barrier, total)


def pick(choices):
    return tuple(slice(None) if choice is None else choice for choice in choices)


def add_blocks(target, parts, shape):
    total = 1
    for size in shape:
        total *= size
    sizes = shape

    def split(index):
        places = []
        for size in reversed(sizes):
            places.append(lax.rem(index, size))
            index = lax.div(index, size)
        return tuple(reversed(places))

    def body(index, carry):
        places = split(index)
        value = parts[0](places).astype(jnp.float32)
        for part in parts[1:]:
            value = value + part(places).astype(jnp.float32)
        target(places, value)
        return carry

    if total == 1:
        body(0, 0)
    else:
        lax.fori_loop(0, total, body, 0)


def scatter_begin(links, order, stage, source, slots):
    axis = order[stage]
    left = [a for a in range(3) if a not in order[:stage]]
    copies = []
    for step in range(1, links.dims[axis]):
        other, device = links.peer(axis, step)
        index = pick([other if a == axis else None for a in left])
        part = source.at[index] if isinstance(index, tuple) else source
        copies.append(links.send(part, slots.at[step - 1], {"ctx": device}))
    return copies


def scatter_end(links, order, stage, copies, source, slots, store):
    axis = order[stage]
    left = [a for a in range(3) if a not in order[:stage]]
    keep = [a for a in left if a != axis]
    for copy in copies:
        copy.wait_recv()

    def own(places):
        where = dict(zip(keep, places))
        where[axis] = links.coords[axis]
        return source[tuple(where[a] for a in left)]

    def arrived(step):
        return lambda places: slots[(step, *places)]

    parts = [own] + [arrived(step) for step in range(links.dims[axis] - 1)]
    add_blocks(store, parts, tuple(links.dims[a] for a in keep))


def gather_begin(links, order, stage, held):
    axis = order[stage]
    whole = order[stage + 1 :]
    index = pick([None if a in whole else links.coords[a] for a in range(3)])
    copies = []
    for step in range(1, links.dims[axis]):
        _, device = links.peer(axis, step)
        copies.append(links.send(held.at[index], held.at[index], {"ctx": device}))
    return copies


def stage_shapes(dims, order, tail):
    slots, sums = [], []
    for stage in range(3):
        axis = order[stage]
        keep = tuple(dims[a] for a in range(3) if a not in order[: stage + 1])
        slots.append((dims[axis] - 1, *keep, *tail))
        if stage < 2:
            sums.append((*keep, *tail))
    return slots, sums


def copies_needed(dims):
    return sum(size - 1 for size in dims)


def run_scatter(links, sources, slots, sums, finals, ready=None):
    pending = []
    for chunk in range(CHUNKS):
        if ready is not None:
            ready(chunk)
        pending.append(scatter_begin(links, ORDERS[chunk], 0, sources[chunk], slots[chunk][0]))
    current = list(sources)
    for stage in range(3):
        for chunk in range(CHUNKS):
            order = ORDERS[chunk]
            if stage < 2:
                target = sums[chunk][stage]

                def store(places, value, target=target):
                    if places:
                        target[places] = value.astype(target.dtype)
                    else:
                        target[...] = value.astype(target.dtype)
            else:
                store = finals[chunk]
            scatter_end(
                links, order, stage, pending[chunk], current[chunk], slots[chunk][stage], store
            )
            if stage < 2:
                current[chunk] = sums[chunk][stage]
                pending[chunk] = scatter_begin(
                    links, order, stage + 1, current[chunk], slots[chunk][stage + 1]
                )


def run_gather(links, helds):
    pending = [None] * CHUNKS
    for stage in (2, 1, 0):
        for chunk in range(CHUNKS):
            if pending[chunk] is not None:
                for copy in pending[chunk]:
                    copy.wait_recv()
            pending[chunk] = gather_begin(links, ORDERS[chunk], stage, helds[chunk])
    for chunk in range(CHUNKS):
        for copy in pending[chunk]:
            copy.wait_recv()


def gather_weights_begin(links, fsdp_count, shards, fulls, local_sem):
    mine = lax.axis_index("fsdp")
    copies, own = [], []
    for place, (shard, full) in enumerate(zip(shards, fulls)):
        for step in range(1, fsdp_count):
            device = lax.rem(mine + step, fsdp_count)
            copies.append(links.send(shard, full.at[mine], {"fsdp": device}))
        copy = pltpu.make_async_copy(shard, full.at[mine], local_sem.at[place])
        copy.start()
        own.append(copy)
    return copies, own


def weights_kernel(count, fsdp_count, dims, *refs):
    shards, fulls = refs[:count], refs[count : 2 * count]
    send_sem, recv_sem, local_sem = refs[2 * count :]
    links = Links(send_sem, recv_sem, dims)
    barrier = pltpu.get_barrier_semaphore()
    mine = lax.axis_index("fsdp")
    for step in range(1, fsdp_count):
        device = lax.rem(mine + step, fsdp_count)
        pl.semaphore_signal(barrier, inc=1, device_id={"fsdp": device}, device_id_type=MESH)
    pl.semaphore_wait(barrier, fsdp_count - 1)
    copies, own = gather_weights_begin(links, fsdp_count, shards, fulls, local_sem)
    for copy in own:
        copy.wait()
    for copy in copies:
        copy.wait_recv()
    links.finish()


def gather_weights(shards, fsdp_count, dims, collective_id):
    count = len(shards)
    total = count * max(fsdp_count - 1, 1)
    fulls = pl.pallas_call(
        functools.partial(weights_kernel, count, fsdp_count, dims),
        out_shape=[jax.ShapeDtypeStruct((fsdp_count, *s.shape), s.dtype) for s in shards],
        in_specs=[pl.BlockSpec(memory_space=pl.ANY)] * count,
        out_specs=[pl.BlockSpec(memory_space=pl.ANY)] * count,
        scratch_shapes=[
            pltpu.SemaphoreType.DMA((total,)),
            pltpu.SemaphoreType.DMA((total,)),
            pltpu.SemaphoreType.DMA((count,)),
        ],
        compiler_params=pltpu.CompilerParams(collective_id=collective_id, has_side_effects=True),
        name="gather_weights",
    )(*shards)
    return [full.reshape(-1, full.shape[-1]) for full in fulls]


def kv_gather_kernel(count, fsdp_count, dims, *refs):
    kv, shards = refs[0], refs[1 : 1 + count]
    held, fulls = refs[1 + count], refs[2 + count : 2 + 2 * count]
    send_sem, recv_sem, local_sem = refs[2 + 2 * count :]
    links = Links(send_sem, recv_sem, dims)
    greet(links, fsdp_count)
    for chunk in range(CHUNKS):
        held[(chunk, *links.coords)] = kv[chunk]
    copies, own = gather_weights_begin(links, fsdp_count, shards, fulls, local_sem)
    run_gather(links, [held.at[chunk] for chunk in range(CHUNKS)])
    for copy in own:
        copy.wait()
    for copy in copies:
        copy.wait_recv()
    links.finish()


def gather_kv(kv, shards, fsdp_count, dims, collective_id):
    count = len(shards)
    total = count * (fsdp_count - 1) + CHUNKS * copies_needed(dims)
    results = pl.pallas_call(
        functools.partial(kv_gather_kernel, count, fsdp_count, dims),
        out_shape=[jax.ShapeDtypeStruct((CHUNKS, *dims, *kv.shape[1:]), kv.dtype)]
        + [jax.ShapeDtypeStruct((fsdp_count, *s.shape), s.dtype) for s in shards],
        in_specs=[pl.BlockSpec(memory_space=pltpu.VMEM)]
        + [pl.BlockSpec(memory_space=pl.ANY)] * count,
        out_specs=[pl.BlockSpec(memory_space=pltpu.VMEM)]
        + [pl.BlockSpec(memory_space=pl.ANY)] * count,
        scratch_shapes=[
            pltpu.SemaphoreType.DMA((total,)),
            pltpu.SemaphoreType.DMA((total,)),
            pltpu.SemaphoreType.DMA((count,)),
        ],
        compiler_params=pltpu.CompilerParams(
            collective_id=collective_id, has_side_effects=True, vmem_limit_bytes=32 << 20
        ),
        name="gather_kv",
    )(kv, *shards)
    return results[0], [full.reshape(-1, full.shape[-1]) for full in results[1:]]


def kv_scatter_kernel(dims, *refs):
    parts, out = refs[0], refs[1]
    refs = refs[2:]
    slots = [refs[5 * c : 5 * c + 3] for c in range(CHUNKS)]
    sums = [refs[5 * c + 3 : 5 * c + 5] for c in range(CHUNKS)]
    send_sem, recv_sem = refs[5 * CHUNKS :]
    links = Links(send_sem, recv_sem, dims)
    greet(links, 1)

    def final(chunk):
        def store(places, value):
            out[chunk] = value

        return store

    run_scatter(
        links,
        [parts.at[chunk] for chunk in range(CHUNKS)],
        slots,
        sums,
        [final(chunk) for chunk in range(CHUNKS)],
    )
    links.finish()


def scatter_scratch(dims, tail):
    scratch = []
    for order in ORDERS:
        slots, sums = stage_shapes(dims, order, tail)
        scratch += [pltpu.VMEM(shape, jnp.bfloat16) for shape in slots + sums]
    return scratch


def scatter_kv(parts, dims, collective_id):
    tail = parts.shape[-2:]
    total = CHUNKS * copies_needed(dims)
    return pl.pallas_call(
        functools.partial(kv_scatter_kernel, dims),
        out_shape=jax.ShapeDtypeStruct((CHUNKS, *tail), jnp.float32),
        in_specs=[pl.BlockSpec(memory_space=pltpu.VMEM)],
        out_specs=pl.BlockSpec(memory_space=pltpu.VMEM),
        scratch_shapes=scatter_scratch(dims, tail)
        + [pltpu.SemaphoreType.DMA((total,)), pltpu.SemaphoreType.DMA((total,))],
        compiler_params=pltpu.CompilerParams(
            collective_id=collective_id, has_side_effects=True, vmem_limit_bytes=32 << 20
        ),
        name="scatter_kv",
    )(parts)


def sum_grads_kernel(fsdp_count, dims, *refs):
    grads, out = refs[0], refs[1]
    arrived, current = refs[2], refs[3]
    refs = refs[4:]
    slots = [refs[5 * c : 5 * c + 3] for c in range(CHUNKS)]
    sums = [refs[5 * c + 3 : 5 * c + 5] for c in range(CHUNKS)]
    send_sem, recv_sem = refs[5 * CHUNKS :]
    links = Links(send_sem, recv_sem, dims)
    greet(links, fsdp_count)
    mine = lax.axis_index("fsdp")
    first = []
    for chunk in range(CHUNKS):
        first.append([])
        for step in range(1, fsdp_count):
            device = lax.rem(mine + step, fsdp_count)
            first[chunk].append(
                links.send(
                    grads.at[device, chunk], arrived.at[step - 1, chunk], {"fsdp": device}
                )
            )

    def ready(chunk):
        for copy in first[chunk]:
            copy.wait_recv()

        def store(places, value):
            current[(chunk, *places)] = value.astype(current.dtype)

        parts = [lambda places: grads[(mine, chunk, *places)]]
        for step in range(fsdp_count - 1):
            parts.append(lambda places, step=step: arrived[(step, chunk, *places)])
        add_blocks(store, parts, dims)

    def final(chunk):
        def store(places, value):
            out[(chunk, *links.coords)] = value.astype(out.dtype)

        return store

    run_scatter(
        links,
        [current.at[chunk] for chunk in range(CHUNKS)],
        slots,
        sums,
        [final(chunk) for chunk in range(CHUNKS)],
        ready,
    )
    run_gather(links, [out.at[chunk] for chunk in range(CHUNKS)])
    links.finish()


def sum_grads(grads, fsdp_count, dims, collective_id):
    tail = grads.shape[-2:]
    total = CHUNKS * (2 * copies_needed(dims) + fsdp_count - 1)
    return pl.pallas_call(
        functools.partial(sum_grads_kernel, fsdp_count, dims),
        out_shape=jax.ShapeDtypeStruct((CHUNKS, *dims, *tail), grads.dtype),
        in_specs=[pl.BlockSpec(memory_space=pltpu.VMEM)],
        out_specs=pl.BlockSpec(memory_space=pltpu.VMEM),
        scratch_shapes=[
            pltpu.VMEM((max(fsdp_count - 1, 1), CHUNKS, *dims, *tail), grads.dtype),
            pltpu.VMEM((CHUNKS, *dims, *tail), grads.dtype),
        ]
        + scatter_scratch(dims, tail)
        + [pltpu.SemaphoreType.DMA((total,)), pltpu.SemaphoreType.DMA((total,))],
        compiler_params=pltpu.CompilerParams(
            collective_id=collective_id, has_side_effects=True, vmem_limit_bytes=48 << 20
        ),
        name="sum_grads",
    )(grads)


def make_tables(positions):
    half_dim = HEAD_DIM // 2
    frequency = theta_base ** (-2.0 * jnp.arange(half_dim, dtype=jnp.float32) / HEAD_DIM)
    angles = positions.astype(jnp.float32)[:, None] * frequency[None, :]
    return (jnp.cos(angles), jnp.sin(angles))


def rotate(values, cosine, sine):
    half_dim = values.shape[-1] // 2
    first_half = values[..., :half_dim]
    second_half = values[..., half_dim:]
    cos_rows = cosine[:, None, :]
    sin_rows = sine[:, None, :]
    return jnp.concatenate(
        [
            first_half * cos_rows - second_half * sin_rows,
            second_half * cos_rows + first_half * sin_rows,
        ],
        axis=-1,
    )


def rotate_back(grads, cosine, sine):
    half_dim = grads.shape[-1] // 2
    first_half = grads[..., :half_dim]
    second_half = grads[..., half_dim:]
    cos_rows = cosine[:, None, :]
    sin_rows = sine[:, None, :]
    return jnp.concatenate(
        [
            first_half * cos_rows + second_half * sin_rows,
            second_half * cos_rows - first_half * sin_rows,
        ],
        axis=-1,
    )


def slot_positions(block_of_slot, offset, count_rows, half_len):
    row_ids = offset + jnp.arange(count_rows, dtype=jnp.int32)
    slot_ids = row_ids // half_len
    slot_match = slot_ids[:, None] == jnp.arange(block_of_slot.shape[0], dtype=jnp.int32)[None, :]
    owners = jnp.sum(jnp.where(slot_match, block_of_slot[None, :], 0), axis=1)
    return owners * half_len + row_ids % half_len


def norm_forward(values, gain_vec):
    inverse = lax.rsqrt(jnp.mean(values * values, axis=-1, keepdims=True) + epsilon)
    scaled = values * inverse
    return (scaled * gain_vec, scaled, inverse)


def norm_backward(grad_output, gain_vec, scaled, inverse):
    grad_scaled = grad_output * gain_vec
    grad_input = inverse * (
        grad_scaled - scaled * jnp.mean(grad_scaled * scaled, axis=-1, keepdims=True)
    )
    grad_gain = jnp.sum(grad_output * scaled, axis=0)
    return (grad_input, grad_gain)


def local(
    x_in,
    w_query,
    w_key,
    w_value,
    w_out,
    attn_gain,
    w_gate,
    w_up,
    w_down,
    mlp_gain,
    block_of_slot,
    out_grad,
):
    fsdp_count = lax.axis_size("fsdp")
    dims = ctx_dims(lax.axis_size("ctx"))
    full_query, full_key, full_value, gain_attn = gather_weights(
        [w_query, w_key, w_value, attn_gain.reshape(1, -1)], fsdp_count, dims, 0
    )
    gain_attn = gain_attn.reshape(-1)
    gain_attn_f = gain_attn.astype(jnp.float32)
    seq_count, tok_count, model_width = x_in.shape
    group_size = HEADS // KV_HEADS
    half_len = tok_count // 2
    rows_all = seq_count * tok_count
    ctx_count = lax.axis_size("ctx")
    score_scale = HEAD_DIM ** (-0.5)
    my_offset = lax.axis_index("ctx") * tok_count
    query_pos = slot_positions(block_of_slot, my_offset, tok_count, half_len)
    cosine, sine = make_tables(query_pos)
    inputs = x_in.astype(jnp.float32).reshape(rows_all, model_width)
    normed_f, scaled_one, inverse_one = norm_forward(inputs, gain_attn_f)
    normed = normed_f.astype(jnp.bfloat16)
    query_f = jnp.dot(normed, full_query, preferred_element_type=jnp.float32).reshape(
        seq_count, tok_count, HEADS, HEAD_DIM
    )
    queries = (
        rotate(query_f, cosine, sine)
        .astype(jnp.bfloat16)
        .reshape(seq_count, tok_count, KV_HEADS, group_size, HEAD_DIM)
    )
    key_f = jnp.dot(normed, full_key, preferred_element_type=jnp.float32).reshape(
        seq_count, tok_count, KV_HEADS, HEAD_DIM
    )
    key_rows = rotate(key_f, cosine, sine).astype(jnp.bfloat16)
    value_rows = (
        jnp.dot(normed, full_value, preferred_element_type=jnp.float32)
        .astype(jnp.bfloat16)
        .reshape(seq_count, tok_count, KV_HEADS, HEAD_DIM)
    )
    kv_rows = (
        jnp.concatenate([key_rows, value_rows], axis=-1)
        .reshape(rows_all, KV_HEADS, 2 * HEAD_DIM)
        .transpose(1, 0, 2)
    )
    kv_all, (full_out, full_gate, full_up, full_down, gain_mlp) = gather_kv(
        kv_rows, [w_out, w_gate, w_up, w_down, mlp_gain.reshape(1, -1)], fsdp_count, dims, 1
    )
    gain_mlp_f = gain_mlp.reshape(-1).astype(jnp.float32)
    kv_all = (
        kv_all.reshape(KV_HEADS, ctx_count, seq_count, tok_count, 2 * HEAD_DIM)
        .transpose(2, 0, 1, 3, 4)
        .reshape(seq_count, KV_HEADS, ctx_count * tok_count, 2 * HEAD_DIM)
    )
    key_all = kv_all[..., :HEAD_DIM]
    value_all = kv_all[..., HEAD_DIM:]
    queries = queries.transpose(0, 2, 3, 1, 4).reshape(
        seq_count, KV_HEADS, group_size * tok_count, HEAD_DIM
    )
    key_pos = slot_positions(block_of_slot, jnp.int32(0), ctx_count * tok_count, half_len)
    visible = jnp.tile(query_pos, group_size)[:, None] >= key_pos[None, :]
    scores = (
        jnp.einsum("skqd,sknd->skqn", queries, key_all, preferred_element_type=jnp.float32)
        * score_scale
    )
    scores = jnp.where(visible, scores, masked_value)
    top = jnp.max(scores, axis=-1, keepdims=True)
    weights = jnp.where(visible, jnp.exp(scores - top), 0.0)
    weights = weights / jnp.sum(weights, axis=-1, keepdims=True)
    weights_low = weights.astype(jnp.bfloat16)
    attended_f = jnp.einsum(
        "skqn,sknd->skqd", weights_low, value_all, preferred_element_type=jnp.float32
    )
    attended = (
        attended_f.astype(jnp.bfloat16)
        .reshape(seq_count, HEADS, tok_count, HEAD_DIM)
        .transpose(0, 2, 1, 3)
        .reshape(rows_all, model_width)
    )
    hidden_state = inputs + jnp.dot(attended, full_out, preferred_element_type=jnp.float32)
    normed_two_f, scaled_two, inverse_two = norm_forward(hidden_state, gain_mlp_f)
    normed_two = normed_two_f.astype(jnp.bfloat16)
    gate_vals = jnp.dot(normed_two, full_gate, preferred_element_type=jnp.float32)
    up_vals = jnp.dot(normed_two, full_up, preferred_element_type=jnp.float32)
    sigmoid_gate = jax.nn.sigmoid(gate_vals)
    activated = gate_vals * sigmoid_gate
    inner_rows = (activated * up_vals).astype(jnp.bfloat16)
    result = hidden_state + jnp.dot(inner_rows, full_down, preferred_element_type=jnp.float32)
    y_out = result.reshape(seq_count, tok_count, model_width).astype(jnp.bfloat16)
    grad_top = out_grad.reshape(rows_all, model_width)
    grad_residual = grad_top.astype(jnp.float32)
    grad_wdown = jnp.einsum("rf,rd->fd", inner_rows, grad_top, preferred_element_type=jnp.float32)
    grad_inner = jnp.einsum("rd,fd->rf", grad_top, full_down, preferred_element_type=jnp.float32)
    grad_gate = (
        grad_inner * up_vals * sigmoid_gate * (1.0 + gate_vals * (1.0 - sigmoid_gate))
    ).astype(jnp.bfloat16)
    grad_up = (grad_inner * activated).astype(jnp.bfloat16)
    grad_wgate = jnp.einsum("rd,rf->df", normed_two, grad_gate, preferred_element_type=jnp.float32)
    grad_wup = jnp.einsum("rd,rf->df", normed_two, grad_up, preferred_element_type=jnp.float32)
    grad_normed_two = jnp.einsum(
        "rf,df->rd", grad_gate, full_gate, preferred_element_type=jnp.float32
    ) + jnp.einsum("rf,df->rd", grad_up, full_up, preferred_element_type=jnp.float32)
    grad_hidden_norm, grad_gain_mlp = norm_backward(
        grad_normed_two, gain_mlp_f, scaled_two, inverse_two
    )
    grad_hidden = grad_residual + grad_hidden_norm
    grad_branch = grad_hidden.astype(jnp.bfloat16)
    grad_wout = jnp.einsum("ri,rj->ij", attended, grad_branch, preferred_element_type=jnp.float32)
    grad_attended = jnp.einsum(
        "rj,ij->ri", grad_branch, full_out, preferred_element_type=jnp.float32
    ).astype(jnp.bfloat16)
    grad_heads = (
        grad_attended.reshape(seq_count, tok_count, HEADS, HEAD_DIM)
        .transpose(0, 2, 1, 3)
        .reshape(seq_count, KV_HEADS, group_size * tok_count, HEAD_DIM)
    )
    row_delta = jnp.sum(grad_heads.astype(jnp.float32) * attended_f, axis=-1, keepdims=True)
    grad_value_part = jnp.einsum(
        "skqn,skqd->sknd", weights_low, grad_heads, preferred_element_type=jnp.float32
    )
    grad_weights = jnp.einsum(
        "skqd,sknd->skqn", grad_heads, value_all, preferred_element_type=jnp.float32
    )
    grad_scores = (weights * (grad_weights - row_delta)).astype(jnp.bfloat16)
    grad_query = jnp.einsum(
        "skqn,sknd->skqd", grad_scores, key_all, preferred_element_type=jnp.float32
    )
    grad_key_part = (
        jnp.einsum("skqn,skqd->sknd", grad_scores, queries, preferred_element_type=jnp.float32)
        * score_scale
    )
    grad_kv_part = (
        jnp.concatenate([grad_key_part, grad_value_part], axis=-1)
        .astype(jnp.bfloat16)
        .reshape(seq_count, KV_HEADS, ctx_count, tok_count, 2 * HEAD_DIM)
        .transpose(1, 2, 0, 3, 4)
        .reshape(KV_HEADS, *dims, rows_all, 2 * HEAD_DIM)
    )
    grad_kv = (
        scatter_kv(grad_kv_part, dims, 2)
        .transpose(1, 0, 2)
        .reshape(seq_count, tok_count, KV_HEADS, 2 * HEAD_DIM)
    )
    grad_key = grad_kv[..., :HEAD_DIM]
    grad_value = grad_kv[..., HEAD_DIM:]
    grad_query_rows = (
        (grad_query * score_scale)
        .reshape(seq_count, HEADS, tok_count, HEAD_DIM)
        .transpose(0, 2, 1, 3)
    )
    grad_query_low = (
        rotate_back(grad_query_rows, cosine, sine)
        .astype(jnp.bfloat16)
        .reshape(rows_all, model_width)
    )
    grad_key_low = (
        rotate_back(grad_key, cosine, sine)
        .astype(jnp.bfloat16)
        .reshape(rows_all, KV_HEADS * HEAD_DIM)
    )
    grad_value_low = grad_value.astype(jnp.bfloat16).reshape(rows_all, KV_HEADS * HEAD_DIM)
    grad_wquery = jnp.einsum(
        "rd,re->de", normed, grad_query_low, preferred_element_type=jnp.float32
    )
    grad_wkey = jnp.einsum("rd,re->de", normed, grad_key_low, preferred_element_type=jnp.float32)
    grad_wvalue = jnp.einsum(
        "rd,re->de", normed, grad_value_low, preferred_element_type=jnp.float32
    )
    grad_normed = jnp.einsum(
        "re,de->rd", grad_query_low, full_query, preferred_element_type=jnp.float32
    )
    grad_normed = grad_normed + jnp.einsum(
        "re,de->rd", grad_key_low, full_key, preferred_element_type=jnp.float32
    )
    grad_normed = grad_normed + jnp.einsum(
        "re,de->rd", grad_value_low, full_value, preferred_element_type=jnp.float32
    )
    grad_input_norm, grad_gain_attn = norm_backward(
        grad_normed, gain_attn_f, scaled_one, inverse_one
    )
    x_grad = (
        (grad_hidden + grad_input_norm)
        .astype(jnp.bfloat16)
        .reshape(seq_count, tok_count, model_width)
    )
    shard_rows = model_width // fsdp_count
    wide = [grad_wquery, grad_wkey, grad_wvalue, grad_wout, grad_wgate, grad_wup]
    widths = [grad.shape[1] for grad in wide]
    columns = jnp.concatenate([grad.astype(jnp.bfloat16) for grad in wide], axis=1)
    wide_tiles = columns.shape[1] // LANES
    columns = columns.reshape(fsdp_count, shard_rows, wide_tiles, LANES).transpose(0, 2, 1, 3)
    hidden = grad_wdown.shape[0]
    half_hidden = hidden // (2 * fsdp_count)
    down_tiles = 2 * model_width // LANES
    down = (
        grad_wdown.astype(jnp.bfloat16)
        .reshape(fsdp_count, 2, half_hidden, model_width)
        .transpose(0, 2, 1, 3)
        .reshape(fsdp_count, half_hidden, down_tiles, LANES)
        .transpose(0, 2, 1, 3)
        .reshape(fsdp_count, -1, shard_rows, LANES)
    )
    tiles = jnp.concatenate([columns, down], axis=1)
    gains = (
        jnp.stack([grad_gain_attn, grad_gain_mlp])
        .astype(jnp.bfloat16)
        .reshape(2, fsdp_count, shard_rows)
        .transpose(1, 0, 2)
        .reshape(fsdp_count, 2 * shard_rows)
    )
    used_tiles = tiles.shape[1]
    tile_count = used_tiles + -used_tiles % (CHUNKS * ctx_count)
    tiles = jnp.pad(tiles, ((0, 0), (0, tile_count - used_tiles), (0, 0), (0, 0)))
    gains = jnp.pad(gains, ((0, 0), (0, EXTRA_ROWS * LANES - 2 * shard_rows)))
    gains = jnp.pad(
        gains.reshape(fsdp_count, 1, EXTRA_ROWS, LANES),
        ((0, 0), (0, tile_count - 1), (0, 0), (0, 0)),
    )
    packed = jnp.concatenate([tiles, gains], axis=2).reshape(
        fsdp_count, CHUNKS, *dims, shard_rows + EXTRA_ROWS, LANES
    )
    summed = sum_grads(packed, fsdp_count, dims, 3).reshape(
        tile_count, shard_rows + EXTRA_ROWS, LANES
    )
    gains = summed[0, shard_rows:].astype(jnp.float32).reshape(-1)
    columns = (
        summed[:wide_tiles, :shard_rows]
        .transpose(1, 0, 2)
        .reshape(shard_rows, wide_tiles * LANES)
        .astype(jnp.float32)
    )
    owned, offset = [], 0
    for width in widths:
        owned.append(columns[:, offset : offset + width])
        offset += width
    down = (
        summed[wide_tiles:used_tiles, :shard_rows]
        .reshape(down_tiles, half_hidden, LANES)
        .transpose(1, 0, 2)
        .reshape(half_hidden, 2, model_width)
        .transpose(1, 0, 2)
        .reshape(2 * half_hidden, model_width)
        .astype(jnp.float32)
    )
    return (
        y_out,
        x_grad,
        owned[0],
        owned[1],
        owned[2],
        owned[3],
        gains[:shard_rows],
        owned[4],
        owned[5],
        down,
        gains[shard_rows : 2 * shard_rows],
    )


def solution(mesh):
    placed = (
        P("fsdp", "ctx", None),
        P("fsdp", None),
        P("fsdp", None),
        P("fsdp", None),
        P("fsdp", None),
        P("fsdp"),
        P("fsdp", None),
        P("fsdp", None),
        P("fsdp", None),
        P("fsdp"),
        P(),
        P("fsdp", "ctx", None),
    )
    return jax.shard_map(
        local,
        mesh=mesh,
        in_specs=placed,
        out_specs=(
            P("fsdp", "ctx", None),
            P("fsdp", "ctx", None),
            P("fsdp", None),
            P("fsdp", None),
            P("fsdp", None),
            P("fsdp", None),
            P("fsdp"),
            P("fsdp", None),
            P("fsdp", None),
            P("fsdp", None),
            P("fsdp"),
        ),
        check_vma=False,
    )
```

```python
import functools

import jax
import jax.numpy as jnp
from jax import lax
from jax.experimental import pallas as pl
from jax.experimental.pallas import tpu as pltpu
from jax.sharding import PartitionSpec as P

HEADS = 9
KV_HEADS = 3
HEAD_DIM = 64
LANES = 128
CHUNKS = 3

epsilon = 1e-05
theta_base = 100000.0
masked_value = -1e30
MESH = pl.DeviceIdType.MESH

ORDERS = ((0, 2, 1), (2, 1, 0), (1, 2, 0), (2, 1, 0), (1, 2, 0), (2, 1, 0))
PIECES = len(ORDERS)


def piece_rows(rows):
    first = (rows + 31) // 32 * 16
    return ((0, first), (first, rows - first))


def piece_of(ref, piece, rows, lead=3):
    start, count = piece_rows(rows)[piece % 2]
    return ref.at[(piece // 2, *[slice(None)] * lead, pl.ds(start, count))]


def ctx_dims(count):
    return (count // 4, 2, 2)


class Links:
    def __init__(self, send_sem, recv_sem, dims):
        self.send_sem = send_sem
        self.recv_sem = recv_sem
        self.dims = dims
        self.me = lax.axis_index("ctx")
        self.strides = (dims[1] * dims[2], dims[2], 1)
        self.coords = tuple(
            lax.rem(lax.div(self.me, stride), size) for stride, size in zip(self.strides, dims)
        )
        self.used = 0
        self.copies = []

    def peer(self, axis, step):
        size = self.dims[axis]
        other = lax.rem(self.coords[axis] + step, size)
        return other, self.me + (other - self.coords[axis]) * self.strides[axis]

    def send(self, source, target, device_id):
        copy = pltpu.make_async_remote_copy(
            src_ref=source,
            dst_ref=target,
            send_sem=self.send_sem.at[self.used],
            recv_sem=self.recv_sem.at[self.used],
            device_id=device_id,
            device_id_type=MESH,
        )
        copy.start()
        self.used += 1
        self.copies.append(copy)
        return copy

    def finish(self):
        for copy in self.copies:
            copy.wait_send()


def greet(links, fsdp_count):
    barrier = pltpu.get_barrier_semaphore()
    total = 0
    for axis in range(3):
        for step in range(1, links.dims[axis]):
            _, device = links.peer(axis, step)
            pl.semaphore_signal(barrier, inc=1, device_id={"ctx": device}, device_id_type=MESH)
            total += 1
    mine = lax.axis_index("fsdp")
    for step in range(1, fsdp_count):
        device = lax.rem(mine + step, fsdp_count)
        pl.semaphore_signal(barrier, inc=1, device_id={"fsdp": device}, device_id_type=MESH)
        total += 1
    pl.semaphore_wait(barrier, total)


def pick(choices):
    return tuple(slice(None) if choice is None else choice for choice in choices)


def add_blocks(target, parts, shape):
    total = 1
    for size in shape:
        total *= size
    sizes = shape

    def split(index):
        places = []
        for size in reversed(sizes):
            places.append(lax.rem(index, size))
            index = lax.div(index, size)
        return tuple(reversed(places))

    def body(index, carry):
        places = split(index)
        value = parts[0](places).astype(jnp.float32)
        for part in parts[1:]:
            value = value + part(places).astype(jnp.float32)
        target(places, value)
        return carry

    if total == 1:
        body(0, 0)
    else:
        lax.fori_loop(0, total, body, 0)


def scatter_begin(links, order, stage, source, slots):
    axis = order[stage]
    left = [a for a in range(3) if a not in order[:stage]]
    copies = []
    for step in range(1, links.dims[axis]):
        other, device = links.peer(axis, step)
        index = pick([other if a == axis else None for a in left])
        part = source.at[index] if isinstance(index, tuple) else source
        copies.append(links.send(part, slots.at[step - 1], {"ctx": device}))
    return copies


def scatter_end(links, order, stage, copies, source, slots, store):
    axis = order[stage]
    left = [a for a in range(3) if a not in order[:stage]]
    keep = [a for a in left if a != axis]
    for copy in copies:
        copy.wait_recv()

    def own(places):
        where = dict(zip(keep, places))
        where[axis] = links.coords[axis]
        return source[tuple(where[a] for a in left)]

    def arrived(step):
        return lambda places: slots[(step, *places)]

    parts = [own] + [arrived(step) for step in range(links.dims[axis] - 1)]
    add_blocks(store, parts, tuple(links.dims[a] for a in keep))


def gather_begin(links, order, stage, held):
    axis = order[stage]
    whole = order[stage + 1 :]
    index = pick([None if a in whole else links.coords[a] for a in range(3)])
    copies = []
    for step in range(1, links.dims[axis]):
        _, device = links.peer(axis, step)
        copies.append(links.send(held.at[index], held.at[index], {"ctx": device}))
    return copies


def stage_shapes(dims, order, tail):
    slots, sums = [], []
    for stage in range(3):
        axis = order[stage]
        keep = tuple(dims[a] for a in range(3) if a not in order[: stage + 1])
        slots.append((dims[axis] - 1, *keep, *tail))
        if stage < 2:
            sums.append((*keep, *tail))
    return slots, sums


def copies_needed(dims):
    return sum(size - 1 for size in dims)


def run_scatter(links, sources, slots, sums, finals, ready=None):
    pending = []
    for chunk in range(PIECES):
        if ready is not None:
            ready(chunk)
        pending.append(scatter_begin(links, ORDERS[chunk], 0, sources[chunk], slots[chunk][0]))
    current = list(sources)
    for stage in range(3):
        for chunk in range(PIECES):
            order = ORDERS[chunk]
            if stage < 2:
                target = sums[chunk][stage]

                def store(places, value, target=target):
                    if places:
                        target[places] = value.astype(target.dtype)
                    else:
                        target[...] = value.astype(target.dtype)
            else:
                store = finals[chunk]
            scatter_end(
                links, order, stage, pending[chunk], current[chunk], slots[chunk][stage], store
            )
            if stage < 2:
                current[chunk] = sums[chunk][stage]
                pending[chunk] = scatter_begin(
                    links, order, stage + 1, current[chunk], slots[chunk][stage + 1]
                )


def run_gather(links, helds):
    pending = [None] * PIECES
    for stage in (2, 1, 0):
        for chunk in range(PIECES):
            if pending[chunk] is not None:
                for copy in pending[chunk]:
                    copy.wait_recv()
            pending[chunk] = gather_begin(links, ORDERS[chunk], stage, helds[chunk])
    for chunk in range(PIECES):
        for copy in pending[chunk]:
            copy.wait_recv()


def gather_weights_begin(links, fsdp_count, shards, fulls, local_sem):
    mine = lax.axis_index("fsdp")
    copies, own = [], []
    for place, (shard, full) in enumerate(zip(shards, fulls)):
        for step in range(1, fsdp_count):
            device = lax.rem(mine + step, fsdp_count)
            copies.append(links.send(shard, full.at[mine], {"fsdp": device}))
        copy = pltpu.make_async_copy(shard, full.at[mine], local_sem.at[place])
        copy.start()
        own.append(copy)
    return copies, own


def weights_kernel(count, fsdp_count, dims, *refs):
    shards, fulls = refs[:count], refs[count : 2 * count]
    send_sem, recv_sem, local_sem = refs[2 * count :]
    links = Links(send_sem, recv_sem, dims)
    barrier = pltpu.get_barrier_semaphore()
    mine = lax.axis_index("fsdp")
    for step in range(1, fsdp_count):
        device = lax.rem(mine + step, fsdp_count)
        pl.semaphore_signal(barrier, inc=1, device_id={"fsdp": device}, device_id_type=MESH)
    pl.semaphore_wait(barrier, fsdp_count - 1)
    copies, own = gather_weights_begin(links, fsdp_count, shards, fulls, local_sem)
    for copy in own:
        copy.wait()
    for copy in copies:
        copy.wait_recv()
    links.finish()


def gather_weights(shards, fsdp_count, dims, collective_id):
    count = len(shards)
    total = count * max(fsdp_count - 1, 1)
    fulls = pl.pallas_call(
        functools.partial(weights_kernel, count, fsdp_count, dims),
        out_shape=[jax.ShapeDtypeStruct((fsdp_count, *s.shape), s.dtype) for s in shards],
        in_specs=[pl.BlockSpec(memory_space=pl.ANY)] * count,
        out_specs=[pl.BlockSpec(memory_space=pl.ANY)] * count,
        scratch_shapes=[
            pltpu.SemaphoreType.DMA((total,)),
            pltpu.SemaphoreType.DMA((total,)),
            pltpu.SemaphoreType.DMA((count,)),
        ],
        compiler_params=pltpu.CompilerParams(collective_id=collective_id, has_side_effects=True),
        name="gather_weights",
    )(*shards)
    return [full.reshape(-1, full.shape[-1]) for full in fulls]


def kv_gather_kernel(count, fsdp_count, dims, *refs):
    kv, shards = refs[0], refs[1 : 1 + count]
    held, fulls = refs[1 + count], refs[2 + count : 2 + 2 * count]
    send_sem, recv_sem, local_sem = refs[2 + 2 * count :]
    links = Links(send_sem, recv_sem, dims)
    greet(links, fsdp_count)
    for chunk in range(CHUNKS):
        held[(chunk, *links.coords)] = kv[chunk]
    copies, own = gather_weights_begin(links, fsdp_count, shards, fulls, local_sem)
    run_gather(links, [piece_of(held, piece, kv.shape[1]) for piece in range(PIECES)])
    for copy in own:
        copy.wait()
    for copy in copies:
        copy.wait_recv()
    links.finish()


def gather_kv(kv, shards, fsdp_count, dims, collective_id):
    count = len(shards)
    total = count * (fsdp_count - 1) + PIECES * copies_needed(dims)
    results = pl.pallas_call(
        functools.partial(kv_gather_kernel, count, fsdp_count, dims),
        out_shape=[jax.ShapeDtypeStruct((CHUNKS, *dims, *kv.shape[1:]), kv.dtype)]
        + [jax.ShapeDtypeStruct((fsdp_count, *s.shape), s.dtype) for s in shards],
        in_specs=[pl.BlockSpec(memory_space=pltpu.VMEM)]
        + [pl.BlockSpec(memory_space=pl.ANY)] * count,
        out_specs=[pl.BlockSpec(memory_space=pltpu.VMEM)]
        + [pl.BlockSpec(memory_space=pl.ANY)] * count,
        scratch_shapes=[
            pltpu.SemaphoreType.DMA((total,)),
            pltpu.SemaphoreType.DMA((total,)),
            pltpu.SemaphoreType.DMA((count,)),
        ],
        compiler_params=pltpu.CompilerParams(
            collective_id=collective_id, has_side_effects=True, vmem_limit_bytes=32 << 20
        ),
        name="gather_kv",
    )(kv, *shards)
    return results[0], [full.reshape(-1, full.shape[-1]) for full in results[1:]]


def kv_scatter_kernel(dims, *refs):
    parts, out = refs[0], refs[1]
    refs = refs[2:]
    slots = [refs[5 * c : 5 * c + 3] for c in range(PIECES)]
    sums = [refs[5 * c + 3 : 5 * c + 5] for c in range(PIECES)]
    send_sem, recv_sem = refs[5 * PIECES :]
    links = Links(send_sem, recv_sem, dims)
    greet(links, 1)

    rows = parts.shape[-2]

    def final(piece):
        target = piece_of(out, piece, rows, 0)

        def store(places, value):
            target[...] = value

        return store

    run_scatter(
        links,
        [piece_of(parts, piece, rows) for piece in range(PIECES)],
        slots,
        sums,
        [final(piece) for piece in range(PIECES)],
    )
    links.finish()


def scatter_scratch(dims, tail):
    scratch = []
    for piece, order in enumerate(ORDERS):
        count = piece_rows(tail[0])[piece % 2][1]
        slots, sums = stage_shapes(dims, order, (count, tail[1]))
        scratch += [pltpu.VMEM(shape, jnp.bfloat16) for shape in slots + sums]
    return scratch


def scatter_kv(parts, dims, collective_id):
    tail = parts.shape[-2:]
    total = PIECES * copies_needed(dims)
    return pl.pallas_call(
        functools.partial(kv_scatter_kernel, dims),
        out_shape=jax.ShapeDtypeStruct((CHUNKS, *tail), jnp.float32),
        in_specs=[pl.BlockSpec(memory_space=pltpu.VMEM)],
        out_specs=pl.BlockSpec(memory_space=pltpu.VMEM),
        scratch_shapes=scatter_scratch(dims, tail)
        + [pltpu.SemaphoreType.DMA((total,)), pltpu.SemaphoreType.DMA((total,))],
        compiler_params=pltpu.CompilerParams(
            collective_id=collective_id, has_side_effects=True, vmem_limit_bytes=32 << 20
        ),
        name="scatter_kv",
    )(parts)


def sum_grads_kernel(fsdp_count, dims, *refs):
    grads, out = refs[0], refs[1]
    arrived, current = refs[2], refs[3]
    refs = refs[4:]
    slots = [refs[5 * c : 5 * c + 3] for c in range(PIECES)]
    sums = [refs[5 * c + 3 : 5 * c + 5] for c in range(PIECES)]
    send_sem, recv_sem = refs[5 * PIECES :]
    links = Links(send_sem, recv_sem, dims)
    greet(links, fsdp_count)
    mine = lax.axis_index("fsdp")
    rows = grads.shape[-2]
    first = []
    for piece in range(PIECES):
        first.append([])
        for step in range(1, fsdp_count):
            device = lax.rem(mine + step, fsdp_count)
            first[piece].append(
                links.send(
                    piece_of(grads.at[device], piece, rows),
                    piece_of(arrived.at[step - 1], piece, rows),
                    {"fsdp": device},
                )
            )

    def ready(piece):
        for copy in first[piece]:
            copy.wait_recv()
        target = piece_of(current, piece, rows)

        def store(places, value):
            target[places] = value.astype(current.dtype)

        views = [piece_of(grads.at[mine], piece, rows)]
        for step in range(fsdp_count - 1):
            views.append(piece_of(arrived.at[step], piece, rows))
        add_blocks(store, [lambda places, view=view: view[places] for view in views], dims)

    def final(piece):
        target = piece_of(out, piece, rows)

        def store(places, value):
            target[links.coords] = value.astype(out.dtype)

        return store

    run_scatter(
        links,
        [piece_of(current, piece, rows) for piece in range(PIECES)],
        slots,
        sums,
        [final(piece) for piece in range(PIECES)],
        ready,
    )
    run_gather(links, [piece_of(out, piece, rows) for piece in range(PIECES)])
    links.finish()


def sum_grads(grads, fsdp_count, dims, collective_id):
    tail = grads.shape[-2:]
    total = PIECES * (2 * copies_needed(dims) + fsdp_count - 1)
    return pl.pallas_call(
        functools.partial(sum_grads_kernel, fsdp_count, dims),
        out_shape=jax.ShapeDtypeStruct((CHUNKS, *dims, *tail), grads.dtype),
        in_specs=[pl.BlockSpec(memory_space=pltpu.VMEM)],
        out_specs=pl.BlockSpec(memory_space=pltpu.VMEM),
        scratch_shapes=[
            pltpu.VMEM((max(fsdp_count - 1, 1), CHUNKS, *dims, *tail), grads.dtype),
            pltpu.VMEM((CHUNKS, *dims, *tail), grads.dtype),
        ]
        + scatter_scratch(dims, tail)
        + [pltpu.SemaphoreType.DMA((total,)), pltpu.SemaphoreType.DMA((total,))],
        compiler_params=pltpu.CompilerParams(
            collective_id=collective_id, has_side_effects=True, vmem_limit_bytes=48 << 20
        ),
        name="sum_grads",
    )(grads)


def pack_kernel(ff_shard, normed, attended, normed_two, top, qkv, branch, gate, up, inner, gains, out):
    fsdp_count, shard_rows, _ = normed.shape
    extra = out.shape[2] - shard_rows

    def product(left, right):
        return jnp.dot(left, right, preferred_element_type=jnp.float32)

    def body(owner, carry):
        def put(tile, value):
            out[owner, tile, :shard_rows, :] = value.astype(out.dtype)
            if tile:
                out[owner, tile, shard_rows:, :] = jnp.zeros((extra, LANES), out.dtype)

        def column(ref, place):
            return ref[:, place * LANES : (place + 1) * LANES]

        out[owner, 0, shard_rows:, :] = gains[owner]
        one, two, three = normed[owner], attended[owner], normed_two[owner]
        tile = 0
        last = qkv.shape[1] // LANES - 1
        for place in range(last):
            put(tile, product(one, column(qkv, place)))
            tile += 1
        put(tile, product(one, column(qkv, last)) + product(two, column(branch, 0)))
        tile += 1
        for place in range(1, branch.shape[1] // LANES):
            put(tile, product(two, column(branch, place)))
            tile += 1
        for ref in (gate, up):
            for place in range(ref.shape[1] // LANES):
                put(tile, product(three, column(ref, place)))
                tile += 1
        for place in range(ff_shard // LANES):
            start = pl.multiple_of(owner * ff_shard + place * LANES, LANES)
            right = inner[:, pl.ds(start, LANES)]
            for part in range(fsdp_count):
                put(tile, product(top[part], right))
                tile += 1
        return carry

    lax.fori_loop(0, fsdp_count, body, 0)


def make_tables(positions):
    half_dim = HEAD_DIM // 2
    frequency = theta_base ** (-2.0 * jnp.arange(half_dim, dtype=jnp.float32) / HEAD_DIM)
    angles = positions.astype(jnp.float32)[:, None] * frequency[None, :]
    return (jnp.cos(angles), jnp.sin(angles))


def rotate(values, cosine, sine):
    half_dim = values.shape[-1] // 2
    first_half = values[..., :half_dim]
    second_half = values[..., half_dim:]
    cos_rows = cosine[:, None, :]
    sin_rows = sine[:, None, :]
    return jnp.concatenate(
        [
            first_half * cos_rows - second_half * sin_rows,
            second_half * cos_rows + first_half * sin_rows,
        ],
        axis=-1,
    )


def rotate_back(grads, cosine, sine):
    half_dim = grads.shape[-1] // 2
    first_half = grads[..., :half_dim]
    second_half = grads[..., half_dim:]
    cos_rows = cosine[:, None, :]
    sin_rows = sine[:, None, :]
    return jnp.concatenate(
        [
            first_half * cos_rows + second_half * sin_rows,
            second_half * cos_rows - first_half * sin_rows,
        ],
        axis=-1,
    )


def slot_positions(block_of_slot, offset, count_rows, half_len):
    row_ids = offset + jnp.arange(count_rows, dtype=jnp.int32)
    slot_ids = row_ids // half_len
    slot_match = slot_ids[:, None] == jnp.arange(block_of_slot.shape[0], dtype=jnp.int32)[None, :]
    owners = jnp.sum(jnp.where(slot_match, block_of_slot[None, :], 0), axis=1)
    return owners * half_len + row_ids % half_len


def norm_forward(values, gain_vec):
    inverse = lax.rsqrt(jnp.mean(values * values, axis=-1, keepdims=True) + epsilon)
    scaled = values * inverse
    return (scaled * gain_vec, scaled, inverse)


def norm_backward(grad_output, gain_vec, scaled, inverse):
    grad_scaled = grad_output * gain_vec
    grad_input = inverse * (
        grad_scaled - scaled * jnp.mean(grad_scaled * scaled, axis=-1, keepdims=True)
    )
    grad_gain = jnp.sum(grad_output * scaled, axis=0)
    return (grad_input, grad_gain)


def local(
    x_in,
    w_query,
    w_key,
    w_value,
    w_out,
    attn_gain,
    w_gate,
    w_up,
    w_down,
    mlp_gain,
    block_of_slot,
    out_grad,
):
    fsdp_count = lax.axis_size("fsdp")
    dims = ctx_dims(lax.axis_size("ctx"))
    full_query, full_key, full_value, gain_attn = gather_weights(
        [w_query, w_key, w_value, attn_gain.reshape(1, -1)], fsdp_count, dims, 0
    )
    gain_attn = gain_attn.reshape(-1)
    gain_attn_f = gain_attn.astype(jnp.float32)
    seq_count, tok_count, model_width = x_in.shape
    group_size = HEADS // KV_HEADS
    half_len = tok_count // 2
    rows_all = seq_count * tok_count
    ctx_count = lax.axis_size("ctx")
    score_scale = HEAD_DIM ** (-0.5)
    my_offset = lax.axis_index("ctx") * tok_count
    query_pos = slot_positions(block_of_slot, my_offset, tok_count, half_len)
    cosine, sine = make_tables(query_pos)
    inputs = x_in.astype(jnp.float32).reshape(rows_all, model_width)
    normed_f, scaled_one, inverse_one = norm_forward(inputs, gain_attn_f)
    normed = normed_f.astype(jnp.bfloat16)
    query_f = jnp.dot(normed, full_query, preferred_element_type=jnp.float32).reshape(
        seq_count, tok_count, HEADS, HEAD_DIM
    )
    queries = (
        rotate(query_f, cosine, sine)
        .astype(jnp.bfloat16)
        .reshape(seq_count, tok_count, KV_HEADS, group_size, HEAD_DIM)
    )
    key_f = jnp.dot(normed, full_key, preferred_element_type=jnp.float32).reshape(
        seq_count, tok_count, KV_HEADS, HEAD_DIM
    )
    key_rows = rotate(key_f, cosine, sine).astype(jnp.bfloat16)
    value_rows = (
        jnp.dot(normed, full_value, preferred_element_type=jnp.float32)
        .astype(jnp.bfloat16)
        .reshape(seq_count, tok_count, KV_HEADS, HEAD_DIM)
    )
    kv_rows = (
        jnp.concatenate([key_rows, value_rows], axis=-1)
        .reshape(rows_all, KV_HEADS, 2 * HEAD_DIM)
        .transpose(1, 0, 2)
    )
    kv_all, (full_out, full_gate, full_up, full_down, gain_mlp) = gather_kv(
        kv_rows, [w_out, w_gate, w_up, w_down, mlp_gain.reshape(1, -1)], fsdp_count, dims, 1
    )
    gain_mlp_f = gain_mlp.reshape(-1).astype(jnp.float32)
    kv_all = (
        kv_all.reshape(KV_HEADS, ctx_count, seq_count, tok_count, 2 * HEAD_DIM)
        .transpose(2, 0, 1, 3, 4)
        .reshape(seq_count, KV_HEADS, ctx_count * tok_count, 2 * HEAD_DIM)
    )
    key_all = kv_all[..., :HEAD_DIM]
    value_all = kv_all[..., HEAD_DIM:]
    queries = queries.transpose(0, 2, 3, 1, 4).reshape(
        seq_count, KV_HEADS, group_size * tok_count, HEAD_DIM
    )
    key_pos = slot_positions(block_of_slot, jnp.int32(0), ctx_count * tok_count, half_len)
    visible = jnp.tile(query_pos, group_size)[:, None] >= key_pos[None, :]
    scores = (
        jnp.einsum("skqd,sknd->skqn", queries, key_all, preferred_element_type=jnp.float32)
        * score_scale
    )
    scores = jnp.where(visible, scores, masked_value)
    top = jnp.max(scores, axis=-1, keepdims=True)
    weights = jnp.where(visible, jnp.exp(scores - top), 0.0)
    weights = weights / jnp.sum(weights, axis=-1, keepdims=True)
    weights_low = weights.astype(jnp.bfloat16)
    attended_f = jnp.einsum(
        "skqn,sknd->skqd", weights_low, value_all, preferred_element_type=jnp.float32
    )
    attended = (
        attended_f.astype(jnp.bfloat16)
        .reshape(seq_count, HEADS, tok_count, HEAD_DIM)
        .transpose(0, 2, 1, 3)
        .reshape(rows_all, model_width)
    )
    hidden_state = inputs + jnp.dot(attended, full_out, preferred_element_type=jnp.float32)
    normed_two_f, scaled_two, inverse_two = norm_forward(hidden_state, gain_mlp_f)
    normed_two = normed_two_f.astype(jnp.bfloat16)
    gate_vals = jnp.dot(normed_two, full_gate, preferred_element_type=jnp.float32)
    up_vals = jnp.dot(normed_two, full_up, preferred_element_type=jnp.float32)
    sigmoid_gate = jax.nn.sigmoid(gate_vals)
    activated = gate_vals * sigmoid_gate
    inner_rows = (activated * up_vals).astype(jnp.bfloat16)
    result = hidden_state + jnp.dot(inner_rows, full_down, preferred_element_type=jnp.float32)
    y_out = result.reshape(seq_count, tok_count, model_width).astype(jnp.bfloat16)
    grad_top = out_grad.reshape(rows_all, model_width)
    grad_residual = grad_top.astype(jnp.float32)
    grad_inner = jnp.einsum("rd,fd->rf", grad_top, full_down, preferred_element_type=jnp.float32)
    grad_gate = (
        grad_inner * up_vals * sigmoid_gate * (1.0 + gate_vals * (1.0 - sigmoid_gate))
    ).astype(jnp.bfloat16)
    grad_up = (grad_inner * activated).astype(jnp.bfloat16)
    grad_normed_two = jnp.einsum(
        "rf,df->rd", grad_gate, full_gate, preferred_element_type=jnp.float32
    ) + jnp.einsum("rf,df->rd", grad_up, full_up, preferred_element_type=jnp.float32)
    grad_hidden_norm, grad_gain_mlp = norm_backward(
        grad_normed_two, gain_mlp_f, scaled_two, inverse_two
    )
    grad_hidden = grad_residual + grad_hidden_norm
    grad_branch = grad_hidden.astype(jnp.bfloat16)
    grad_attended = jnp.einsum(
        "rj,ij->ri", grad_branch, full_out, preferred_element_type=jnp.float32
    ).astype(jnp.bfloat16)
    grad_heads = (
        grad_attended.reshape(seq_count, tok_count, HEADS, HEAD_DIM)
        .transpose(0, 2, 1, 3)
        .reshape(seq_count, KV_HEADS, group_size * tok_count, HEAD_DIM)
    )
    row_delta = jnp.sum(grad_heads.astype(jnp.float32) * attended_f, axis=-1, keepdims=True)
    grad_value_part = jnp.einsum(
        "skqn,skqd->sknd", weights_low, grad_heads, preferred_element_type=jnp.float32
    )
    grad_weights = jnp.einsum(
        "skqd,sknd->skqn", grad_heads, value_all, preferred_element_type=jnp.float32
    )
    grad_scores = (weights * (grad_weights - row_delta)).astype(jnp.bfloat16)
    grad_query = jnp.einsum(
        "skqn,sknd->skqd", grad_scores, key_all, preferred_element_type=jnp.float32
    )
    grad_key_part = (
        jnp.einsum("skqn,skqd->sknd", grad_scores, queries, preferred_element_type=jnp.float32)
        * score_scale
    )
    grad_kv_part = (
        jnp.concatenate([grad_key_part, grad_value_part], axis=-1)
        .astype(jnp.bfloat16)
        .reshape(seq_count, KV_HEADS, ctx_count, tok_count, 2 * HEAD_DIM)
        .transpose(1, 2, 0, 3, 4)
        .reshape(KV_HEADS, *dims, rows_all, 2 * HEAD_DIM)
    )
    grad_kv = (
        scatter_kv(grad_kv_part, dims, 2)
        .transpose(1, 0, 2)
        .reshape(seq_count, tok_count, KV_HEADS, 2 * HEAD_DIM)
    )
    grad_key = grad_kv[..., :HEAD_DIM]
    grad_value = grad_kv[..., HEAD_DIM:]
    grad_query_rows = (
        (grad_query * score_scale)
        .reshape(seq_count, HEADS, tok_count, HEAD_DIM)
        .transpose(0, 2, 1, 3)
    )
    grad_query_low = (
        rotate_back(grad_query_rows, cosine, sine)
        .astype(jnp.bfloat16)
        .reshape(rows_all, model_width)
    )
    grad_key_low = (
        rotate_back(grad_key, cosine, sine)
        .astype(jnp.bfloat16)
        .reshape(rows_all, KV_HEADS * HEAD_DIM)
    )
    grad_value_low = grad_value.astype(jnp.bfloat16).reshape(rows_all, KV_HEADS * HEAD_DIM)
    grad_normed = jnp.einsum(
        "re,de->rd", grad_query_low, full_query, preferred_element_type=jnp.float32
    )
    grad_normed = grad_normed + jnp.einsum(
        "re,de->rd", grad_key_low, full_key, preferred_element_type=jnp.float32
    )
    grad_normed = grad_normed + jnp.einsum(
        "re,de->rd", grad_value_low, full_value, preferred_element_type=jnp.float32
    )
    grad_input_norm, grad_gain_attn = norm_backward(
        grad_normed, gain_attn_f, scaled_one, inverse_one
    )
    x_grad = (
        (grad_hidden + grad_input_norm)
        .astype(jnp.bfloat16)
        .reshape(seq_count, tok_count, model_width)
    )
    shard_rows = model_width // fsdp_count
    extra_rows = 16 + -shard_rows % 16
    hidden = inner_rows.shape[1]
    ff_shard = hidden // fsdp_count
    aligned = ff_shard % LANES == 0
    widths = [model_width, KV_HEADS * HEAD_DIM, KV_HEADS * HEAD_DIM, model_width, hidden, hidden]
    wide_tiles = sum(widths) // LANES
    half_hidden = hidden // (2 * fsdp_count)
    down_tiles = 2 * model_width // LANES
    gains = (
        jnp.stack([grad_gain_attn, grad_gain_mlp])
        .astype(jnp.bfloat16)
        .reshape(2, fsdp_count, shard_rows)
        .transpose(1, 0, 2)
        .reshape(fsdp_count, 2 * shard_rows)
    )
    gains = jnp.pad(gains, ((0, 0), (0, extra_rows * LANES - 2 * shard_rows))).reshape(
        fsdp_count, extra_rows, LANES
    )
    if aligned:
        used_tiles = wide_tiles + ff_shard // LANES * fsdp_count

        def turned(rows):
            return rows.T.reshape(fsdp_count, shard_rows, rows_all)

        blank = jnp.zeros((rows_all, LANES // 2), jnp.bfloat16)
        packed = pl.pallas_call(
            functools.partial(pack_kernel, ff_shard),
            out_shape=jax.ShapeDtypeStruct(
                (fsdp_count, used_tiles, shard_rows + extra_rows, LANES), jnp.bfloat16
            ),
            compiler_params=pltpu.CompilerParams(vmem_limit_bytes=32 << 20),
            name="pack_grads",
        )(
            turned(normed),
            turned(attended),
            turned(normed_two),
            turned(grad_top),
            jnp.concatenate([grad_query_low, grad_key_low, grad_value_low, blank], axis=1),
            jnp.concatenate([blank, grad_branch], axis=1),
            grad_gate,
            grad_up,
            inner_rows,
            gains,
        )
    else:

        def summed_rows(left, right):
            return jnp.einsum("ri,rj->ij", left, right, preferred_element_type=jnp.float32).astype(
                jnp.bfloat16
            )

        columns = jnp.concatenate(
            [
                summed_rows(normed, grad_query_low),
                summed_rows(normed, grad_key_low),
                summed_rows(normed, grad_value_low),
                summed_rows(attended, grad_branch),
                summed_rows(normed_two, grad_gate),
                summed_rows(normed_two, grad_up),
            ],
            axis=1,
        )
        columns = columns.reshape(fsdp_count, shard_rows, wide_tiles, LANES).transpose(0, 2, 1, 3)
        down = (
            summed_rows(inner_rows, grad_top)
            .reshape(fsdp_count, 2, half_hidden, model_width)
            .transpose(0, 2, 1, 3)
            .reshape(fsdp_count, half_hidden, down_tiles, LANES)
            .transpose(0, 2, 1, 3)
            .reshape(fsdp_count, -1, shard_rows, LANES)
        )
        tiles = jnp.concatenate([columns, down], axis=1)
        used_tiles = tiles.shape[1]
        gains = jnp.pad(gains[:, None], ((0, 0), (0, used_tiles - 1), (0, 0), (0, 0)))
        packed = jnp.concatenate([tiles, gains], axis=2)
    tile_count = used_tiles + -used_tiles % (CHUNKS * ctx_count)
    if tile_count != used_tiles:
        packed = jnp.pad(packed, ((0, 0), (0, tile_count - used_tiles), (0, 0), (0, 0)))
    packed = packed.reshape(fsdp_count, CHUNKS, *dims, shard_rows + extra_rows, LANES)
    summed = sum_grads(packed, fsdp_count, dims, 3).reshape(
        tile_count, shard_rows + extra_rows, LANES
    )
    gains = summed[0, shard_rows:].astype(jnp.float32).reshape(-1)
    columns = (
        summed[:wide_tiles, :shard_rows]
        .transpose(1, 0, 2)
        .reshape(shard_rows, wide_tiles * LANES)
        .astype(jnp.float32)
    )
    owned, offset = [], 0
    for width in widths:
        owned.append(columns[:, offset : offset + width])
        offset += width
    down = summed[wide_tiles:used_tiles, :shard_rows]
    if aligned:
        down = down.reshape(-1, fsdp_count, shard_rows, LANES).transpose(0, 3, 1, 2)
    else:
        down = (
            down.reshape(down_tiles, half_hidden, LANES)
            .transpose(1, 0, 2)
            .reshape(half_hidden, 2, model_width)
            .transpose(1, 0, 2)
        )
    down = down.reshape(ff_shard, model_width).astype(jnp.float32)
    return (
        y_out,
        x_grad,
        owned[0],
        owned[1],
        owned[2],
        owned[3],
        gains[:shard_rows],
        owned[4],
        owned[5],
        down,
        gains[shard_rows : 2 * shard_rows],
    )


def solution(mesh):
    placed = (
        P("fsdp", "ctx", None),
        P("fsdp", None),
        P("fsdp", None),
        P("fsdp", None),
        P("fsdp", None),
        P("fsdp"),
        P("fsdp", None),
        P("fsdp", None),
        P("fsdp", None),
        P("fsdp"),
        P(),
        P("fsdp", "ctx", None),
    )
    return jax.shard_map(
        local,
        mesh=mesh,
        in_specs=placed,
        out_specs=(
            P("fsdp", "ctx", None),
            P("fsdp", "ctx", None),
            P("fsdp", None),
            P("fsdp", None),
            P("fsdp", None),
            P("fsdp", None),
            P("fsdp"),
            P("fsdp", None),
            P("fsdp", None),
            P("fsdp", None),
            P("fsdp"),
        ),
        check_vma=False,
    )
```

```python
import functools

import jax
import jax.numpy as jnp
from jax import lax
from jax.experimental import pallas as pl
from jax.experimental.pallas import tpu as pltpu
from jax.sharding import PartitionSpec as P

HEADS = 9
KV_HEADS = 3
HEAD_DIM = 64
LANES = 128
CHUNKS = 3

epsilon = 1e-05
theta_base = 100000.0
masked_value = -1e30
MESH = pl.DeviceIdType.MESH

ORDERS = ((0, 2, 1), (2, 1, 0), (1, 2, 0), (2, 1, 0), (1, 2, 0), (2, 1, 0))
PIECES = len(ORDERS)


def piece_rows(rows):
    first = (rows + 31) // 32 * 16
    return ((0, first), (first, rows - first))


def piece_of(ref, piece, rows, lead=3):
    start, count = piece_rows(rows)[piece % 2]
    return ref.at[(piece // 2, *[slice(None)] * lead, pl.ds(start, count))]


def ctx_dims(count):
    return (count // 4, 2, 2)


class Links:
    def __init__(self, send_sem, recv_sem, dims):
        self.send_sem = send_sem
        self.recv_sem = recv_sem
        self.dims = dims
        self.me = lax.axis_index("ctx")
        self.strides = (dims[1] * dims[2], dims[2], 1)
        self.coords = tuple(
            lax.rem(lax.div(self.me, stride), size) for stride, size in zip(self.strides, dims)
        )
        self.used = 0
        self.copies = []

    def peer(self, axis, step):
        size = self.dims[axis]
        other = lax.rem(self.coords[axis] + step, size)
        return other, self.me + (other - self.coords[axis]) * self.strides[axis]

    def send(self, source, target, device_id):
        copy = pltpu.make_async_remote_copy(
            src_ref=source,
            dst_ref=target,
            send_sem=self.send_sem.at[self.used],
            recv_sem=self.recv_sem.at[self.used],
            device_id=device_id,
            device_id_type=MESH,
        )
        copy.start()
        self.used += 1
        self.copies.append(copy)
        return copy

    def finish(self):
        for copy in self.copies:
            copy.wait_send()


def greet(links, fsdp_count):
    barrier = pltpu.get_barrier_semaphore()
    total = 0
    for axis in range(3):
        for step in range(1, links.dims[axis]):
            _, device = links.peer(axis, step)
            pl.semaphore_signal(barrier, inc=1, device_id={"ctx": device}, device_id_type=MESH)
            total += 1
    mine = lax.axis_index("fsdp")
    for step in range(1, fsdp_count):
        device = lax.rem(mine + step, fsdp_count)
        pl.semaphore_signal(barrier, inc=1, device_id={"fsdp": device}, device_id_type=MESH)
        total += 1
    pl.semaphore_wait(barrier, total)


def pick(choices):
    return tuple(slice(None) if choice is None else choice for choice in choices)


def add_blocks(target, parts, shape):
    total = 1
    for size in shape:
        total *= size
    sizes = shape

    def split(index):
        places = []
        for size in reversed(sizes):
            places.append(lax.rem(index, size))
            index = lax.div(index, size)
        return tuple(reversed(places))

    def body(index, carry):
        places = split(index)
        value = parts[0](places).astype(jnp.float32)
        for part in parts[1:]:
            value = value + part(places).astype(jnp.float32)
        target(places, value)
        return carry

    if total == 1:
        body(0, 0)
    else:
        lax.fori_loop(0, total, body, 0)


def scatter_begin(links, order, stage, source, slots):
    axis = order[stage]
    left = [a for a in range(3) if a not in order[:stage]]
    copies = []
    for step in range(1, links.dims[axis]):
        other, device = links.peer(axis, step)
        index = pick([other if a == axis else None for a in left])
        part = source.at[index] if isinstance(index, tuple) else source
        copies.append(links.send(part, slots.at[step - 1], {"ctx": device}))
    return copies


def scatter_end(links, order, stage, copies, source, slots, store):
    axis = order[stage]
    left = [a for a in range(3) if a not in order[:stage]]
    keep = [a for a in left if a != axis]
    for copy in copies:
        copy.wait_recv()

    def own(places):
        where = dict(zip(keep, places))
        where[axis] = links.coords[axis]
        return source[tuple(where[a] for a in left)]

    def arrived(step):
        return lambda places: slots[(step, *places)]

    parts = [own] + [arrived(step) for step in range(links.dims[axis] - 1)]
    add_blocks(store, parts, tuple(links.dims[a] for a in keep))


def gather_begin(links, order, stage, held):
    axis = order[stage]
    whole = order[stage + 1 :]
    index = pick([None if a in whole else links.coords[a] for a in range(3)])
    copies = []
    for step in range(1, links.dims[axis]):
        _, device = links.peer(axis, step)
        copies.append(links.send(held.at[index], held.at[index], {"ctx": device}))
    return copies


def stage_shapes(dims, order, tail):
    slots, sums = [], []
    for stage in range(3):
        axis = order[stage]
        keep = tuple(dims[a] for a in range(3) if a not in order[: stage + 1])
        slots.append((dims[axis] - 1, *keep, *tail))
        if stage < 2:
            sums.append((*keep, *tail))
    return slots, sums


def copies_needed(dims):
    return sum(size - 1 for size in dims)


def run_scatter(links, sources, slots, sums, finals, ready=None):
    pending = []
    for chunk in range(PIECES):
        if ready is not None:
            ready(chunk)
        pending.append(scatter_begin(links, ORDERS[chunk], 0, sources[chunk], slots[chunk][0]))
    current = list(sources)
    for stage in range(3):
        for chunk in range(PIECES):
            order = ORDERS[chunk]
            if stage < 2:
                target = sums[chunk][stage]

                def store(places, value, target=target):
                    if places:
                        target[places] = value.astype(target.dtype)
                    else:
                        target[...] = value.astype(target.dtype)
            else:
                store = finals[chunk]
            scatter_end(
                links, order, stage, pending[chunk], current[chunk], slots[chunk][stage], store
            )
            if stage < 2:
                current[chunk] = sums[chunk][stage]
                pending[chunk] = scatter_begin(
                    links, order, stage + 1, current[chunk], slots[chunk][stage + 1]
                )


def run_gather(links, helds):
    pending = [None] * PIECES
    for stage in (2, 1, 0):
        for chunk in range(PIECES):
            if pending[chunk] is not None:
                for copy in pending[chunk]:
                    copy.wait_recv()
            pending[chunk] = gather_begin(links, ORDERS[chunk], stage, helds[chunk])
    for chunk in range(PIECES):
        for copy in pending[chunk]:
            copy.wait_recv()


def gather_weights_begin(links, fsdp_count, shards, fulls, local_sem):
    mine = lax.axis_index("fsdp")
    copies, own = [], []
    for place, (shard, full) in enumerate(zip(shards, fulls)):
        for step in range(1, fsdp_count):
            device = lax.rem(mine + step, fsdp_count)
            copies.append(links.send(shard, full.at[mine], {"fsdp": device}))
        copy = pltpu.make_async_copy(shard, full.at[mine], local_sem.at[place])
        copy.start()
        own.append(copy)
    return copies, own


def weights_kernel(count, fsdp_count, dims, *refs):
    shards, fulls = refs[:count], refs[count : 2 * count]
    send_sem, recv_sem, local_sem = refs[2 * count :]
    links = Links(send_sem, recv_sem, dims)
    barrier = pltpu.get_barrier_semaphore()
    mine = lax.axis_index("fsdp")
    for step in range(1, fsdp_count):
        device = lax.rem(mine + step, fsdp_count)
        pl.semaphore_signal(barrier, inc=1, device_id={"fsdp": device}, device_id_type=MESH)
    pl.semaphore_wait(barrier, fsdp_count - 1)
    copies, own = gather_weights_begin(links, fsdp_count, shards, fulls, local_sem)
    for copy in own:
        copy.wait()
    for copy in copies:
        copy.wait_recv()
    links.finish()


def gather_weights(shards, fsdp_count, dims, collective_id):
    count = len(shards)
    total = count * max(fsdp_count - 1, 1)
    fulls = pl.pallas_call(
        functools.partial(weights_kernel, count, fsdp_count, dims),
        out_shape=[jax.ShapeDtypeStruct((fsdp_count, *s.shape), s.dtype) for s in shards],
        in_specs=[pl.BlockSpec(memory_space=pl.ANY)] * count,
        out_specs=[pl.BlockSpec(memory_space=pl.ANY)] * count,
        scratch_shapes=[
            pltpu.SemaphoreType.DMA((total,)),
            pltpu.SemaphoreType.DMA((total,)),
            pltpu.SemaphoreType.DMA((count,)),
        ],
        compiler_params=pltpu.CompilerParams(collective_id=collective_id, has_side_effects=True),
        name="gather_weights",
    )(*shards)
    return [full.reshape(-1, full.shape[-1]) for full in fulls]


def kv_gather_kernel(count, fsdp_count, dims, *refs):
    kv, shards = refs[0], refs[1 : 1 + count]
    held, fulls = refs[1 + count], refs[2 + count : 2 + 2 * count]
    send_sem, recv_sem, local_sem = refs[2 + 2 * count :]
    links = Links(send_sem, recv_sem, dims)
    greet(links, fsdp_count)
    for chunk in range(CHUNKS):
        held[(chunk, *links.coords)] = kv[chunk]
    copies, own = gather_weights_begin(links, fsdp_count, shards, fulls, local_sem)
    run_gather(links, [piece_of(held, piece, kv.shape[1]) for piece in range(PIECES)])
    for copy in own:
        copy.wait()
    for copy in copies:
        copy.wait_recv()
    links.finish()


def gather_kv(kv, shards, fsdp_count, dims, collective_id):
    count = len(shards)
    total = count * (fsdp_count - 1) + PIECES * copies_needed(dims)
    results = pl.pallas_call(
        functools.partial(kv_gather_kernel, count, fsdp_count, dims),
        out_shape=[jax.ShapeDtypeStruct((CHUNKS, *dims, *kv.shape[1:]), kv.dtype)]
        + [jax.ShapeDtypeStruct((fsdp_count, *s.shape), s.dtype) for s in shards],
        in_specs=[pl.BlockSpec(memory_space=pltpu.VMEM)]
        + [pl.BlockSpec(memory_space=pl.ANY)] * count,
        out_specs=[pl.BlockSpec(memory_space=pltpu.VMEM)]
        + [pl.BlockSpec(memory_space=pl.ANY)] * count,
        scratch_shapes=[
            pltpu.SemaphoreType.DMA((total,)),
            pltpu.SemaphoreType.DMA((total,)),
            pltpu.SemaphoreType.DMA((count,)),
        ],
        compiler_params=pltpu.CompilerParams(
            collective_id=collective_id, has_side_effects=True, vmem_limit_bytes=32 << 20
        ),
        name="gather_kv",
    )(kv, *shards)
    return results[0], [full.reshape(-1, full.shape[-1]) for full in results[1:]]


def kv_scatter_kernel(dims, *refs):
    parts, out = refs[0], refs[1]
    refs = refs[2:]
    slots = [refs[5 * c : 5 * c + 3] for c in range(PIECES)]
    sums = [refs[5 * c + 3 : 5 * c + 5] for c in range(PIECES)]
    send_sem, recv_sem = refs[5 * PIECES :]
    links = Links(send_sem, recv_sem, dims)
    greet(links, 1)

    rows = parts.shape[-2]

    def final(piece):
        target = piece_of(out, piece, rows, 0)

        def store(places, value):
            target[...] = value

        return store

    run_scatter(
        links,
        [piece_of(parts, piece, rows) for piece in range(PIECES)],
        slots,
        sums,
        [final(piece) for piece in range(PIECES)],
    )
    links.finish()


def scatter_scratch(dims, tail):
    scratch = []
    for piece, order in enumerate(ORDERS):
        count = piece_rows(tail[0])[piece % 2][1]
        slots, sums = stage_shapes(dims, order, (count, tail[1]))
        scratch += [pltpu.VMEM(shape, jnp.bfloat16) for shape in slots + sums]
    return scratch


def scatter_kv(parts, dims, collective_id):
    tail = parts.shape[-2:]
    total = PIECES * copies_needed(dims)
    return pl.pallas_call(
        functools.partial(kv_scatter_kernel, dims),
        out_shape=jax.ShapeDtypeStruct((CHUNKS, *tail), jnp.float32),
        in_specs=[pl.BlockSpec(memory_space=pltpu.VMEM)],
        out_specs=pl.BlockSpec(memory_space=pltpu.VMEM),
        scratch_shapes=scatter_scratch(dims, tail)
        + [pltpu.SemaphoreType.DMA((total,)), pltpu.SemaphoreType.DMA((total,))],
        compiler_params=pltpu.CompilerParams(
            collective_id=collective_id, has_side_effects=True, vmem_limit_bytes=32 << 20
        ),
        name="scatter_kv",
    )(parts)


def sum_grads_kernel(fsdp_count, dims, *refs):
    grads, out = refs[0], refs[1]
    arrived, current = refs[2], refs[3]
    refs = refs[4:]
    slots = [refs[5 * c : 5 * c + 3] for c in range(PIECES)]
    sums = [refs[5 * c + 3 : 5 * c + 5] for c in range(PIECES)]
    send_sem, recv_sem = refs[5 * PIECES :]
    links = Links(send_sem, recv_sem, dims)
    greet(links, fsdp_count)
    mine = lax.axis_index("fsdp")
    rows = grads.shape[-2]
    first = []
    for piece in range(PIECES):
        first.append([])
        for step in range(1, fsdp_count):
            device = lax.rem(mine + step, fsdp_count)
            first[piece].append(
                links.send(
                    piece_of(grads.at[device], piece, rows),
                    piece_of(arrived.at[step - 1], piece, rows),
                    {"fsdp": device},
                )
            )

    def ready(piece):
        for copy in first[piece]:
            copy.wait_recv()
        target = piece_of(current, piece, rows)

        def store(places, value):
            target[places] = value.astype(current.dtype)

        views = [piece_of(grads.at[mine], piece, rows)]
        for step in range(fsdp_count - 1):
            views.append(piece_of(arrived.at[step], piece, rows))
        add_blocks(store, [lambda places, view=view: view[places] for view in views], dims)

    def final(piece):
        target = piece_of(out, piece, rows)

        def store(places, value):
            target[links.coords] = value.astype(out.dtype)

        return store

    run_scatter(
        links,
        [piece_of(current, piece, rows) for piece in range(PIECES)],
        slots,
        sums,
        [final(piece) for piece in range(PIECES)],
        ready,
    )
    run_gather(links, [piece_of(out, piece, rows) for piece in range(PIECES)])
    links.finish()


def sum_grads(grads, fsdp_count, dims, collective_id):
    tail = grads.shape[-2:]
    total = PIECES * (2 * copies_needed(dims) + fsdp_count - 1)
    return pl.pallas_call(
        functools.partial(sum_grads_kernel, fsdp_count, dims),
        out_shape=jax.ShapeDtypeStruct((CHUNKS, *dims, *tail), grads.dtype),
        in_specs=[pl.BlockSpec(memory_space=pltpu.VMEM)],
        out_specs=pl.BlockSpec(memory_space=pltpu.VMEM),
        scratch_shapes=[
            pltpu.VMEM((max(fsdp_count - 1, 1), CHUNKS, *dims, *tail), grads.dtype),
            pltpu.VMEM((CHUNKS, *dims, *tail), grads.dtype),
        ]
        + scatter_scratch(dims, tail)
        + [pltpu.SemaphoreType.DMA((total,)), pltpu.SemaphoreType.DMA((total,))],
        compiler_params=pltpu.CompilerParams(
            collective_id=collective_id, has_side_effects=True, vmem_limit_bytes=48 << 20
        ),
        name="sum_grads",
    )(grads)


def pack_kernel(ff_shard, normed, attended, normed_two, top, qkv, branch, gate, up, inner, gains, out):
    fsdp_count, shard_rows, _ = normed.shape
    extra = out.shape[2] - shard_rows

    def product(left, right):
        return jnp.dot(left, right, preferred_element_type=jnp.float32)

    def body(owner, carry):
        def put(tile, value):
            out[owner, tile, :shard_rows, :] = value.astype(out.dtype)
            if tile:
                out[owner, tile, shard_rows:, :] = jnp.zeros((extra, LANES), out.dtype)

        def column(ref, place):
            return ref[:, place * LANES : (place + 1) * LANES]

        out[owner, 0, shard_rows:, :] = gains[owner]
        one, two, three = normed[owner], attended[owner], normed_two[owner]
        tile = 0
        last = qkv.shape[1] // LANES - 1
        for place in range(last):
            put(tile, product(one, column(qkv, place)))
            tile += 1
        put(tile, product(one, column(qkv, last)) + product(two, column(branch, 0)))
        tile += 1
        for place in range(1, branch.shape[1] // LANES):
            put(tile, product(two, column(branch, place)))
            tile += 1
        for ref in (gate, up):
            for place in range(ref.shape[1] // LANES):
                put(tile, product(three, column(ref, place)))
                tile += 1
        for place in range(ff_shard // LANES):
            start = pl.multiple_of(owner * ff_shard + place * LANES, LANES)
            right = inner[:, pl.ds(start, LANES)]
            for part in range(fsdp_count):
                put(tile, product(top[part], right))
                tile += 1
        return carry

    lax.fori_loop(0, fsdp_count, body, 0)


def dot_over(left, right, left_dim, right_dim):
    return lax.dot_general(
        left, right, (((left_dim,), (right_dim,)), ((), ())), preferred_element_type=jnp.float32
    )


def keys_values(kv, head, seq):
    block = kv[head, :, seq]
    block = block.reshape(block.shape[0] * block.shape[1], block.shape[2])
    return block[:, :HEAD_DIM], block[:, HEAD_DIM:]


def attention_kernel(queries, kv, query_pos, key_pos, out, log_total):
    visible = query_pos[...] >= key_pos[...]
    for seq in range(queries.shape[0]):
        for head in range(KV_HEADS):
            keys, values = keys_values(kv, head, seq)
            scores = dot_over(queries[seq, head], keys, 1, 1) * HEAD_DIM ** (-0.5)
            scores = jnp.where(visible, scores, masked_value)
            top = jnp.max(scores, axis=-1, keepdims=True)
            weights = jnp.where(visible, jnp.exp(scores - top), 0.0)
            total = jnp.sum(weights, axis=-1, keepdims=True)
            weights = (weights / total).astype(jnp.bfloat16)
            out[seq, head] = jnp.dot(weights, values, preferred_element_type=jnp.float32)
            log_total[seq, head] = top + jnp.log(total)


def attention_grad_kernel(
    queries, kv, query_pos, key_pos, grads, delta, log_total, grad_query, grad_kv
):
    scale = HEAD_DIM ** (-0.5)
    visible = query_pos[...] >= key_pos[...]
    for seq in range(queries.shape[0]):
        for head in range(KV_HEADS):
            keys, values = keys_values(kv, head, seq)
            query, grad = queries[seq, head], grads[seq, head]
            scores = dot_over(query, keys, 1, 1) * scale
            weights = jnp.where(visible, jnp.exp(scores - log_total[seq, head]), 0.0)
            grad_value = dot_over(weights.astype(jnp.bfloat16), grad, 0, 0)
            grad_weights = dot_over(grad, values, 1, 1)
            grad_scores = (weights * (grad_weights - delta[seq, head])).astype(jnp.bfloat16)
            grad_query[seq, head] = jnp.dot(grad_scores, keys, preferred_element_type=jnp.float32)
            grad_key = dot_over(grad_scores, query, 0, 0) * scale
            both = jnp.concatenate([grad_key, grad_value], axis=1).astype(jnp.bfloat16)
            grad_kv[head, :, seq] = both.reshape(kv.shape[1], kv.shape[3], kv.shape[4])


def make_tables(positions):
    half_dim = HEAD_DIM // 2
    frequency = theta_base ** (-2.0 * jnp.arange(half_dim, dtype=jnp.float32) / HEAD_DIM)
    angles = positions.astype(jnp.float32)[:, None] * frequency[None, :]
    return (jnp.cos(angles), jnp.sin(angles))


def rotate(values, cosine, sine):
    half_dim = values.shape[-1] // 2
    first_half = values[..., :half_dim]
    second_half = values[..., half_dim:]
    cos_rows = cosine[:, None, :]
    sin_rows = sine[:, None, :]
    return jnp.concatenate(
        [
            first_half * cos_rows - second_half * sin_rows,
            second_half * cos_rows + first_half * sin_rows,
        ],
        axis=-1,
    )


def rotate_back(grads, cosine, sine):
    half_dim = grads.shape[-1] // 2
    first_half = grads[..., :half_dim]
    second_half = grads[..., half_dim:]
    cos_rows = cosine[:, None, :]
    sin_rows = sine[:, None, :]
    return jnp.concatenate(
        [
            first_half * cos_rows + second_half * sin_rows,
            second_half * cos_rows - first_half * sin_rows,
        ],
        axis=-1,
    )


def slot_positions(block_of_slot, offset, count_rows, half_len):
    row_ids = offset + jnp.arange(count_rows, dtype=jnp.int32)
    slot_ids = row_ids // half_len
    slot_match = slot_ids[:, None] == jnp.arange(block_of_slot.shape[0], dtype=jnp.int32)[None, :]
    owners = jnp.sum(jnp.where(slot_match, block_of_slot[None, :], 0), axis=1)
    return owners * half_len + row_ids % half_len


def norm_forward(values, gain_vec):
    inverse = lax.rsqrt(jnp.mean(values * values, axis=-1, keepdims=True) + epsilon)
    scaled = values * inverse
    return (scaled * gain_vec, scaled, inverse)


def norm_backward(grad_output, gain_vec, scaled, inverse):
    grad_scaled = grad_output * gain_vec
    grad_input = inverse * (
        grad_scaled - scaled * jnp.mean(grad_scaled * scaled, axis=-1, keepdims=True)
    )
    grad_gain = jnp.sum(grad_output * scaled, axis=0)
    return (grad_input, grad_gain)


def local(
    x_in,
    w_query,
    w_key,
    w_value,
    w_out,
    attn_gain,
    w_gate,
    w_up,
    w_down,
    mlp_gain,
    block_of_slot,
    out_grad,
):
    fsdp_count = lax.axis_size("fsdp")
    dims = ctx_dims(lax.axis_size("ctx"))
    full_query, full_key, full_value, gain_attn = gather_weights(
        [w_query, w_key, w_value, attn_gain.reshape(1, -1)], fsdp_count, dims, 0
    )
    gain_attn = gain_attn.reshape(-1)
    gain_attn_f = gain_attn.astype(jnp.float32)
    seq_count, tok_count, model_width = x_in.shape
    group_size = HEADS // KV_HEADS
    half_len = tok_count // 2
    rows_all = seq_count * tok_count
    ctx_count = lax.axis_size("ctx")
    score_scale = HEAD_DIM ** (-0.5)
    my_offset = lax.axis_index("ctx") * tok_count
    query_pos = slot_positions(block_of_slot, my_offset, tok_count, half_len)
    cosine, sine = make_tables(query_pos)
    inputs = x_in.astype(jnp.float32).reshape(rows_all, model_width)
    normed_f, scaled_one, inverse_one = norm_forward(inputs, gain_attn_f)
    normed = normed_f.astype(jnp.bfloat16)
    query_f = jnp.dot(normed, full_query, preferred_element_type=jnp.float32).reshape(
        seq_count, tok_count, HEADS, HEAD_DIM
    )
    queries = (
        rotate(query_f, cosine, sine)
        .astype(jnp.bfloat16)
        .reshape(seq_count, tok_count, KV_HEADS, group_size, HEAD_DIM)
    )
    key_f = jnp.dot(normed, full_key, preferred_element_type=jnp.float32).reshape(
        seq_count, tok_count, KV_HEADS, HEAD_DIM
    )
    key_rows = rotate(key_f, cosine, sine).astype(jnp.bfloat16)
    value_rows = (
        jnp.dot(normed, full_value, preferred_element_type=jnp.float32)
        .astype(jnp.bfloat16)
        .reshape(seq_count, tok_count, KV_HEADS, HEAD_DIM)
    )
    kv_rows = (
        jnp.concatenate([key_rows, value_rows], axis=-1)
        .reshape(rows_all, KV_HEADS, 2 * HEAD_DIM)
        .transpose(1, 0, 2)
    )
    kv_all, (full_out, full_gate, full_up, full_down, gain_mlp) = gather_kv(
        kv_rows, [w_out, w_gate, w_up, w_down, mlp_gain.reshape(1, -1)], fsdp_count, dims, 1
    )
    gain_mlp_f = gain_mlp.reshape(-1).astype(jnp.float32)
    kv_all = kv_all.reshape(KV_HEADS, ctx_count, seq_count, tok_count, 2 * HEAD_DIM)
    queries = queries.transpose(0, 2, 3, 1, 4).reshape(
        seq_count, KV_HEADS, group_size * tok_count, HEAD_DIM
    )
    key_pos = slot_positions(block_of_slot, jnp.int32(0), ctx_count * tok_count, half_len)
    row_pos = jnp.tile(query_pos, group_size)[:, None]
    key_pos = key_pos[None, :]
    local_params = pltpu.CompilerParams(vmem_limit_bytes=40 << 20)
    head_shape = queries.shape
    attended_f, log_total = pl.pallas_call(
        attention_kernel,
        out_shape=[
            jax.ShapeDtypeStruct(head_shape, jnp.float32),
            jax.ShapeDtypeStruct((*head_shape[:-1], 1), jnp.float32),
        ],
        compiler_params=local_params,
        name="attention",
    )(queries, kv_all, row_pos, key_pos)
    attended = (
        attended_f.astype(jnp.bfloat16)
        .reshape(seq_count, HEADS, tok_count, HEAD_DIM)
        .transpose(0, 2, 1, 3)
        .reshape(rows_all, model_width)
    )
    hidden_state = inputs + jnp.dot(attended, full_out, preferred_element_type=jnp.float32)
    normed_two_f, scaled_two, inverse_two = norm_forward(hidden_state, gain_mlp_f)
    normed_two = normed_two_f.astype(jnp.bfloat16)
    gate_vals = jnp.dot(normed_two, full_gate, preferred_element_type=jnp.float32)
    up_vals = jnp.dot(normed_two, full_up, preferred_element_type=jnp.float32)
    sigmoid_gate = jax.nn.sigmoid(gate_vals)
    activated = gate_vals * sigmoid_gate
    inner_rows = (activated * up_vals).astype(jnp.bfloat16)
    result = hidden_state + jnp.dot(inner_rows, full_down, preferred_element_type=jnp.float32)
    y_out = result.reshape(seq_count, tok_count, model_width).astype(jnp.bfloat16)
    grad_top = out_grad.reshape(rows_all, model_width)
    grad_residual = grad_top.astype(jnp.float32)
    grad_inner = jnp.einsum("rd,fd->rf", grad_top, full_down, preferred_element_type=jnp.float32)
    grad_gate = (
        grad_inner * up_vals * sigmoid_gate * (1.0 + gate_vals * (1.0 - sigmoid_gate))
    ).astype(jnp.bfloat16)
    grad_up = (grad_inner * activated).astype(jnp.bfloat16)
    grad_normed_two = jnp.einsum(
        "rf,df->rd", grad_gate, full_gate, preferred_element_type=jnp.float32
    ) + jnp.einsum("rf,df->rd", grad_up, full_up, preferred_element_type=jnp.float32)
    grad_hidden_norm, grad_gain_mlp = norm_backward(
        grad_normed_two, gain_mlp_f, scaled_two, inverse_two
    )
    grad_hidden = grad_residual + grad_hidden_norm
    grad_branch = grad_hidden.astype(jnp.bfloat16)
    grad_attended = jnp.einsum(
        "rj,ij->ri", grad_branch, full_out, preferred_element_type=jnp.float32
    ).astype(jnp.bfloat16)
    grad_heads = (
        grad_attended.reshape(seq_count, tok_count, HEADS, HEAD_DIM)
        .transpose(0, 2, 1, 3)
        .reshape(seq_count, KV_HEADS, group_size * tok_count, HEAD_DIM)
    )
    row_delta = jnp.sum(grad_heads.astype(jnp.float32) * attended_f, axis=-1, keepdims=True)
    grad_query, grad_kv_part = pl.pallas_call(
        attention_grad_kernel,
        out_shape=[
            jax.ShapeDtypeStruct(head_shape, jnp.float32),
            jax.ShapeDtypeStruct(kv_all.shape, jnp.bfloat16),
        ],
        compiler_params=local_params,
        name="attention_grad",
    )(queries, kv_all, row_pos, key_pos, grad_heads, row_delta, log_total)
    grad_kv_part = grad_kv_part.reshape(KV_HEADS, *dims, rows_all, 2 * HEAD_DIM)
    grad_kv = (
        scatter_kv(grad_kv_part, dims, 2)
        .transpose(1, 0, 2)
        .reshape(seq_count, tok_count, KV_HEADS, 2 * HEAD_DIM)
    )
    grad_key = grad_kv[..., :HEAD_DIM]
    grad_value = grad_kv[..., HEAD_DIM:]
    grad_query_rows = (
        (grad_query * score_scale)
        .reshape(seq_count, HEADS, tok_count, HEAD_DIM)
        .transpose(0, 2, 1, 3)
    )
    grad_query_low = (
        rotate_back(grad_query_rows, cosine, sine)
        .astype(jnp.bfloat16)
        .reshape(rows_all, model_width)
    )
    grad_key_low = (
        rotate_back(grad_key, cosine, sine)
        .astype(jnp.bfloat16)
        .reshape(rows_all, KV_HEADS * HEAD_DIM)
    )
    grad_value_low = grad_value.astype(jnp.bfloat16).reshape(rows_all, KV_HEADS * HEAD_DIM)
    grad_normed = jnp.einsum(
        "re,de->rd", grad_query_low, full_query, preferred_element_type=jnp.float32
    )
    grad_normed = grad_normed + jnp.einsum(
        "re,de->rd", grad_key_low, full_key, preferred_element_type=jnp.float32
    )
    grad_normed = grad_normed + jnp.einsum(
        "re,de->rd", grad_value_low, full_value, preferred_element_type=jnp.float32
    )
    grad_input_norm, grad_gain_attn = norm_backward(
        grad_normed, gain_attn_f, scaled_one, inverse_one
    )
    x_grad = (
        (grad_hidden + grad_input_norm)
        .astype(jnp.bfloat16)
        .reshape(seq_count, tok_count, model_width)
    )
    shard_rows = model_width // fsdp_count
    extra_rows = 16 + -shard_rows % 16
    hidden = inner_rows.shape[1]
    ff_shard = hidden // fsdp_count
    aligned = ff_shard % LANES == 0
    widths = [model_width, KV_HEADS * HEAD_DIM, KV_HEADS * HEAD_DIM, model_width, hidden, hidden]
    wide_tiles = sum(widths) // LANES
    half_hidden = hidden // (2 * fsdp_count)
    down_tiles = 2 * model_width // LANES
    gains = (
        jnp.stack([grad_gain_attn, grad_gain_mlp])
        .astype(jnp.bfloat16)
        .reshape(2, fsdp_count, shard_rows)
        .transpose(1, 0, 2)
        .reshape(fsdp_count, 2 * shard_rows)
    )
    gains = jnp.pad(gains, ((0, 0), (0, extra_rows * LANES - 2 * shard_rows))).reshape(
        fsdp_count, extra_rows, LANES
    )
    if aligned:
        used_tiles = wide_tiles + ff_shard // LANES * fsdp_count

        def turned(rows):
            return rows.T.reshape(fsdp_count, shard_rows, rows_all)

        blank = jnp.zeros((rows_all, LANES // 2), jnp.bfloat16)
        packed = pl.pallas_call(
            functools.partial(pack_kernel, ff_shard),
            out_shape=jax.ShapeDtypeStruct(
                (fsdp_count, used_tiles, shard_rows + extra_rows, LANES), jnp.bfloat16
            ),
            compiler_params=pltpu.CompilerParams(vmem_limit_bytes=32 << 20),
            name="pack_grads",
        )(
            turned(normed),
            turned(attended),
            turned(normed_two),
            turned(grad_top),
            jnp.concatenate([grad_query_low, grad_key_low, grad_value_low, blank], axis=1),
            jnp.concatenate([blank, grad_branch], axis=1),
            grad_gate,
            grad_up,
            inner_rows,
            gains,
        )
    else:

        def summed_rows(left, right):
            return jnp.einsum("ri,rj->ij", left, right, preferred_element_type=jnp.float32).astype(
                jnp.bfloat16
            )

        columns = jnp.concatenate(
            [
                summed_rows(normed, grad_query_low),
                summed_rows(normed, grad_key_low),
                summed_rows(normed, grad_value_low),
                summed_rows(attended, grad_branch),
                summed_rows(normed_two, grad_gate),
                summed_rows(normed_two, grad_up),
            ],
            axis=1,
        )
        columns = columns.reshape(fsdp_count, shard_rows, wide_tiles, LANES).transpose(0, 2, 1, 3)
        down = (
            summed_rows(inner_rows, grad_top)
            .reshape(fsdp_count, 2, half_hidden, model_width)
            .transpose(0, 2, 1, 3)
            .reshape(fsdp_count, half_hidden, down_tiles, LANES)
            .transpose(0, 2, 1, 3)
            .reshape(fsdp_count, -1, shard_rows, LANES)
        )
        tiles = jnp.concatenate([columns, down], axis=1)
        used_tiles = tiles.shape[1]
        gains = jnp.pad(gains[:, None], ((0, 0), (0, used_tiles - 1), (0, 0), (0, 0)))
        packed = jnp.concatenate([tiles, gains], axis=2)
    tile_count = used_tiles + -used_tiles % (CHUNKS * ctx_count)
    if tile_count != used_tiles:
        packed = jnp.pad(packed, ((0, 0), (0, tile_count - used_tiles), (0, 0), (0, 0)))
    packed = packed.reshape(fsdp_count, CHUNKS, *dims, shard_rows + extra_rows, LANES)
    summed = sum_grads(packed, fsdp_count, dims, 3).reshape(
        tile_count, shard_rows + extra_rows, LANES
    )
    gains = summed[0, shard_rows:].astype(jnp.float32).reshape(-1)
    columns = (
        summed[:wide_tiles, :shard_rows]
        .transpose(1, 0, 2)
        .reshape(shard_rows, wide_tiles * LANES)
        .astype(jnp.float32)
    )
    owned, offset = [], 0
    for width in widths:
        owned.append(columns[:, offset : offset + width])
        offset += width
    down = summed[wide_tiles:used_tiles, :shard_rows]
    if aligned:
        down = down.reshape(-1, fsdp_count, shard_rows, LANES).transpose(0, 3, 1, 2)
    else:
        down = (
            down.reshape(down_tiles, half_hidden, LANES)
            .transpose(1, 0, 2)
            .reshape(half_hidden, 2, model_width)
            .transpose(1, 0, 2)
        )
    down = down.reshape(ff_shard, model_width).astype(jnp.float32)
    return (
        y_out,
        x_grad,
        owned[0],
        owned[1],
        owned[2],
        owned[3],
        gains[:shard_rows],
        owned[4],
        owned[5],
        down,
        gains[shard_rows : 2 * shard_rows],
    )


def solution(mesh):
    placed = (
        P("fsdp", "ctx", None),
        P("fsdp", None),
        P("fsdp", None),
        P("fsdp", None),
        P("fsdp", None),
        P("fsdp"),
        P("fsdp", None),
        P("fsdp", None),
        P("fsdp", None),
        P("fsdp"),
        P(),
        P("fsdp", "ctx", None),
    )
    return jax.shard_map(
        local,
        mesh=mesh,
        in_specs=placed,
        out_specs=(
            P("fsdp", "ctx", None),
            P("fsdp", "ctx", None),
            P("fsdp", None),
            P("fsdp", None),
            P("fsdp", None),
            P("fsdp", None),
            P("fsdp"),
            P("fsdp", None),
            P("fsdp", None),
            P("fsdp", None),
            P("fsdp"),
        ),
        check_vma=False,
    )
```
